128 devices in a mesh: ctx: 16 (over z, x), head: 8 (over y, core).
Axes of the slice: x: 4, y: 4, z: 4, core: 2. Of those that a mesh axis runs over, the one named last changes fastest.
Arguments:
- queries: bfloat16 [4096, 2048], P('ctx', 'head'), may hold values from -110 to 110
- keys: bfloat16 [65536, 128], P('ctx'), may hold values from -6 to 6
- values: bfloat16 [65536, 128], P('ctx'), may hold values from -6 to 6
- w_out: bfloat16 [2048, 16384], P(None, 'head'), may hold values from -0.125 to 0.125
- new_counts: int32 [8], replicated, may hold values from 1 to 2048, as said below
- prior_lengths: int32 [8], replicated, may hold values from 1 to 30720, as said below
Outputs:
- mixed: bfloat16 [4096, 16384], P('ctx', 'head')
The draws below stay inside these ranges and needn't reach their ends.
Inputs may be any that keep to these rules, and one draw needn't show every extreme that they name: `new_counts`: every request has at least one new token; the counts add up to 4096. `prior_lengths`: every request has at least one cached token; the lengths add up to 61440.
All inputs are finite; a program needn't handle non-finite values.
Results may differ from the reference program's by a relative error of at most 0.011.
Values may be sent and summed in bfloat16 or wider, within the bound.
A program may use at most 384 MiB of HBM per device.

```python
import jax
import jax.numpy as jnp
from jax import lax

D = 16384
HD = 128
HEADS = 16
QD = 256
CK = 4096
REQS = 8
QTOT = 4096
KTOT = 65536


def draw_queries(key, part):
    key = jax.random.fold_in(key, 11)
    first = jax.random.fold_in(key, 0)
    base = jnp.clip(jax.random.normal(first, (QTOT, HEADS, HD), jnp.float32), -6.0, 6.0)
    return base.reshape(QTOT, HEADS * HD).astype(jnp.bfloat16)


def draw_keys(key, part):
    key = jax.random.fold_in(key, 12)
    base = jnp.clip(jax.random.normal(key, (KTOT, HD), jnp.float32), -6.0, 6.0)
    return base.astype(jnp.bfloat16)


def request_layout(key):
    long_slot = jax.random.randint(jax.random.fold_in(key, 21), (), 1, REQS - 4).astype(jnp.int32)
    slot_index = jnp.arange(REQS, dtype=jnp.int32)
    lead_mask = (slot_index < long_slot).astype(jnp.int32)
    tail_mask = ((slot_index > long_slot) & (slot_index <= long_slot + 3)).astype(jnp.int32)
    trail_mask = (slot_index > long_slot + 3).astype(jnp.int32)
    long_mask = (slot_index == long_slot).astype(jnp.int32)
    return (long_mask, lead_mask, tail_mask, trail_mask)


def share_total(key, amount, slot_mask):
    slot_index = jnp.arange(REQS, dtype=jnp.int32)
    shares = jax.random.randint(key, (REQS,), 1, 9).astype(jnp.int32) * slot_mask
    share_sum = jnp.sum(shares)
    spare = amount - jnp.sum(slot_mask)
    base = spare * shares // share_sum
    leftover = spare - jnp.sum(base)
    first_slot = jnp.min(jnp.where(slot_mask > 0, slot_index, REQS))
    return (slot_mask + base + leftover * (slot_index == first_slot).astype(jnp.int32)).astype(jnp.int32)


def draw_new_counts(key, part):
    long_mask, lead_mask, tail_mask, trail_mask = request_layout(key)
    key = jax.random.fold_in(key, 22)
    first, second, third, fourth, fifth = jax.random.split(key, 5)
    tail_new = jax.random.randint(first, (REQS,), 1, QD // 8 + 1).astype(jnp.int32) * tail_mask
    whole_blocks = jax.random.randint(second, (), 0, QTOT // (2 * QD) - 1).astype(jnp.int32)
    offset = jax.random.randint(third, (), QD // 4, QD // 2 + 1).astype(jnp.int32)
    lead_total = QD * whole_blocks + offset
    lead_new = share_total(fourth, lead_total, lead_mask)
    trail_total = QTOT // 2 - jnp.sum(tail_new) - lead_total
    trail_new = share_total(fifth, trail_total, trail_mask)
    long_new = QTOT // 2 * long_mask
    return (lead_new + long_new + tail_new + trail_new).astype(jnp.int32)


def draw_prior_lengths(key, part):
    long_mask, lead_mask, tail_mask, trail_mask = request_layout(key)
    key = jax.random.fold_in(key, 23)
    first, second = jax.random.split(key, 2)
    side_prior = jax.random.randint(first, (REQS,), 1, CK // 8 + 1).astype(jnp.int32) * (lead_mask + trail_mask)
    long_prior = (KTOT - QTOT) // 2 * long_mask
    tail_total = KTOT - QTOT - (KTOT - QTOT) // 2 - jnp.sum(side_prior)
    tail_prior = share_total(second, tail_total, tail_mask)
    return (side_prior + long_prior + tail_prior).astype(jnp.int32)


def block_scale(key, shape, cuts, smallest, largest):
    level, own = 1.0, jax.random.fold_in(key, 6)
    for axis_at, shards_of in cuts:
        steps = jnp.exp(jax.random.uniform(jax.random.fold_in(own, axis_at), (shards_of,), jnp.float32, smallest / len(cuts), largest / len(cuts)))
        level = level * jnp.repeat(steps, shape[axis_at] // shards_of).reshape([-1 if axis == axis_at else 1 for axis in range(len(shape))])
    return level


def gaussian(rng, shape, width, limit, pieces=(), kind=jnp.bfloat16):
    loudness = block_scale(rng, shape, pieces, -0.22, 0.18) if pieces else 1.0
    entries = jax.random.normal(rng, shape, jnp.float32) * width * loudness
    return jnp.minimum(jnp.maximum(entries, -limit), limit).astype(kind)


def setup_inputs(seed: int = 0) -> dict:
    arg_keys = jax.random.split(jax.random.key(seed), 7)
    queries = draw_queries(jax.random.fold_in(arg_keys[6], 71), 0)
    keys = draw_keys(jax.random.fold_in(arg_keys[6], 71), 0)
    values = gaussian(arg_keys[2], (KTOT, HD), 1.0, 6.0, ((0, 16),))
    w_out = gaussian(arg_keys[3], (HEADS * HD, D), (HEADS * HD) ** -0.5, 0.125, ((1, 8),))
    new_counts = draw_new_counts(jax.random.fold_in(arg_keys[6], 71), 0)
    prior_lengths = draw_prior_lengths(jax.random.fold_in(arg_keys[6], 71), 0)
    return {"queries": queries, "keys": keys, "values": values, "w_out": w_out, "new_counts": new_counts, "prior_lengths": prior_lengths}


NEG = -1e30


def row_info(index, ends, table):
    req = jnp.sum((index[:, None] >= ends[None, :]).astype(jnp.int32), axis=1).astype(jnp.int32)
    onehot = (req[:, None] == jnp.arange(ends.shape[0], dtype=jnp.int32)[None, :]).astype(jnp.int32)
    return req, (index + jnp.sum(onehot * table[None, :], axis=1)).astype(jnp.int32)


def reference(queries, keys, values, w_out, new_counts, prior_lengths):
    q_ends = jnp.cumsum(new_counts).astype(jnp.int32)
    q_table = (prior_lengths - (q_ends - new_counts)).astype(jnp.int32)
    spans = (new_counts + prior_lengths).astype(jnp.int32)
    k_ends = jnp.cumsum(spans).astype(jnp.int32)
    k_table = (spans - k_ends).astype(jnp.int32)
    q_req, q_pos = row_info(jnp.arange(QTOT, dtype=jnp.int32), q_ends, q_table)
    k_req, k_pos = row_info(jnp.arange(KTOT, dtype=jnp.int32), k_ends, k_table)
    keys_wide = keys.astype(jnp.float32)
    values_wide = values.astype(jnp.float32)
    blocks = queries.reshape(QTOT // 64, 64, HEADS, HD)

    def one_block(item):
        q_block, b_req, b_pos = item
        scores = jnp.einsum("nhd,kd->nhk", q_block.astype(jnp.float32), keys_wide) * (HD ** -0.5)
        allowed = ((b_req[:, None] == k_req[None, :]) & (k_pos[None, :] <= b_pos[:, None]))[:, None, :]
        scores = jnp.where(allowed, scores, NEG)
        top = jnp.max(scores, axis=2)
        weights = jnp.where(allowed, jnp.exp(scores - top[:, :, None]), 0.0)
        total = jnp.sum(weights, axis=2)
        rounded = lax.optimization_barrier(weights.astype(jnp.bfloat16))
        summed = jnp.einsum("nhk,kd->nhd", rounded.astype(jnp.float32), values_wide)
        return summed / total[:, :, None]

    attended = lax.map(one_block, (blocks, q_req.reshape(-1, 64), q_pos.reshape(-1, 64)))
    attended = attended.reshape(QTOT, HEADS * HD).astype(jnp.bfloat16)
    return jnp.dot(attended, w_out, preferred_element_type=jnp.float32).astype(jnp.bfloat16)
```

```python
import functools
import math

import jax
import jax.numpy as jnp
from jax import lax
from jax.experimental import pallas as pl
from jax.experimental.pallas import tpu as pltpu
from jax.sharding import PartitionSpec as P

MESH = pl.DeviceIdType.MESH
CTX = 16
HEAD = 8
SIDE = 4
REQS = 8
HALF = 128
WIDTH = 128
HEADS = 2
LANES = HALF * HEADS
KEYS = 4096
PIECE = KEYS // HEAD
TILE = 512
SUB = 256
SUMS = 16
LOW = -1e9
NEG = -1e30
LARGE = 2.0**100
SCALE = math.log2(math.e) / math.sqrt(WIDTH)
VMEM = 56 * 1024 * 1024


def remote(src, dst, send, recv, ctx, head):
    return pltpu.make_async_remote_copy(
        src_ref=src, dst_ref=dst, send_sem=send, recv_sem=recv, device_id=(ctx, head), device_id_type=MESH
    )


def greet(peers):
    barrier = pltpu.get_barrier_semaphore()
    for ctx, head in peers:
        pl.semaphore_signal(barrier, inc=1, device_id=(ctx, head), device_id_type=MESH)
    pl.semaphore_wait(barrier, len(peers))


def dispatch_kernel(
    q_ref, k_ref, v_ref, qg_ref, ko_ref, vo_ref, own_sem, qz_send, qx_send, q_recv, kz_send, ky_send, kc_send, k_recv
):
    ctx, head = lax.axis_index("ctx"), lax.axis_index("head")
    z, x = ctx // SIDE, ctx % SIDE
    y, core = head // 2, head % 2
    far = lax.rem(ctx + CTX // 2, CTX)
    twin = y * 2 + (1 - core)

    def zed(d):
        return lax.rem(z + d, SIDE)

    def on_x(d):
        return z * SIDE + lax.rem(x + d, SIDE)

    def on_y(d):
        return lax.rem(y + d, SIDE) * 2 + core

    greet(
        [(zed(d) * SIDE + x, head) for d in (1, 2, 3)]
        + [(on_x(d), head) for d in (1, 2, 3)]
        + [(ctx, on_y(d)) for d in (1, 2, 3)]
        + [(ctx, twin)]
    )
    cache = (k_ref, v_ref)
    far_cache = (ko_ref, vo_ref)
    pending = []

    def start(copy):
        copy.start()
        pending.append(copy)
        return copy

    def piece(ref, p):
        return ref.at[pl.ds(p * PIECE, PIECE), :]

    def rows(zt):
        return q_ref.at[pl.ds((zt // 2) * HALF, HALF), :]

    def share_q(slot, src, turn):
        for d in (1, 3, 2):
            start(remote(src, qg_ref.at[slot], qx_send.at[turn, d - 1], q_recv.at[slot], on_x(d), head))

    for i in range(2):
        start(remote(piece(cache[i], head), piece(far_cache[i], head), kz_send.at[i], k_recv.at[i, head], far, head))
    for d in (1, 3, 2):
        zt = zed(d)
        start(remote(rows(zt), qg_ref.at[ctx], qz_send.at[d - 1], q_recv.at[ctx], zt * SIDE + x, head))
    own = pltpu.make_async_copy(rows(z), qg_ref.at[ctx], own_sem)
    own.start()
    share_q(ctx, rows(z), 0)

    def arrived_q(slot):
        remote(qg_ref.at[slot], qg_ref.at[slot], qz_send.at[0], q_recv.at[slot], ctx, head).wait_recv()

    def arrived_kv(i, p):
        ref = piece(far_cache[i], p)
        remote(ref, ref, kz_send.at[0], k_recv.at[i, p], ctx, head).wait_recv()

    def pass_q(d):
        slot = zed(d) * SIDE + x
        arrived_q(slot)
        share_q(slot, qg_ref.at[slot], d)

    def pass_kv(i):
        arrived_kv(i, head)
        ref = piece(far_cache[i], head)
        for d in (1, 3, 2):
            start(remote(ref, ref, ky_send.at[i, d - 1], k_recv.at[i, head], ctx, on_y(d)))
        start(remote(ref, ref, kc_send.at[i, 0], k_recv.at[i, head], ctx, twin))

    pass_q(1)
    pass_q(3)
    pass_kv(0)
    pass_q(2)
    pass_kv(1)
    for i in range(2):
        for d in (1, 3, 2):
            p = on_y(d)
            arrived_kv(i, p)
            ref = piece(far_cache[i], p)
            start(remote(ref, ref, kc_send.at[i, d], k_recv.at[i, p], ctx, twin))
    for dx in (1, 2, 3):
        for dz in range(SIDE):
            arrived_q(zed(dz) * SIDE + lax.rem(x + dx, SIDE))
    for i in range(2):
        for d in range(SIDE):
            arrived_kv(i, lax.rem(y + d, SIDE) * 2 + (1 - core))
    own.wait()
    for copy in pending:
        copy.wait_send()


def dispatch(queries, keys, values):
    anywhere = pl.BlockSpec(memory_space=pl.ANY)
    dma = pltpu.SemaphoreType.DMA
    return pl.pallas_call(
        dispatch_kernel,
        out_shape=(
            jax.ShapeDtypeStruct((CTX, HALF, LANES), queries.dtype),
            jax.ShapeDtypeStruct(keys.shape, keys.dtype),
            jax.ShapeDtypeStruct(values.shape, values.dtype),
        ),
        in_specs=[anywhere] * 3,
        out_specs=(anywhere,) * 3,
        scratch_shapes=[
            dma,
            dma((3,)),
            dma((SIDE, 3)),
            dma((CTX,)),
            dma((2,)),
            dma((2, 3)),
            dma((2, SIDE)),
            dma((2, HEAD)),
        ],
        compiler_params=pltpu.CompilerParams(collective_id=0, has_side_effects=True),
        name="dispatch",
    )(queries, keys, values)


def attend_kernel(new_ref, prior_ref, qg_ref, k_ref, v_ref, ko_ref, vo_ref, ot_ref, st_ref, vt_ref, qt_ref, m_ref, acc_ref, bad_ref):
    ctx = lax.axis_index("ctx")
    half = ctx // (CTX // 2)
    far = lax.rem(ctx + CTX // 2, CTX)
    vt_ref[WIDTH:, :] = jnp.ones((SUMS, 2 * KEYS), jnp.bfloat16)
    for part, ref in enumerate((v_ref, vo_ref)):

        @pl.loop(0, KEYS // TILE)
        def _(t):
            at = pl.multiple_of(t * TILE, TILE)
            to = pl.multiple_of(part * KEYS + t * TILE, TILE)
            vt_ref[:WIDTH, pl.ds(to, TILE)] = ref[pl.ds(at, TILE), :].T

    q_start, k_start = [jnp.int32(0)], [jnp.int32(0)]
    for r in range(REQS - 1):
        q_start.append(q_start[-1] + new_ref[r])
        k_start.append(k_start[-1] + new_ref[r] + prior_ref[r])

    def bounds(row):
        lo = jnp.zeros_like(row)
        hi = row + prior_ref[0]
        for r in range(1, REQS):
            here = row >= q_start[r]
            lo = jnp.where(here, k_start[r], lo)
            hi = jnp.where(here, row - q_start[r] + prior_ref[r] + k_start[r], hi)
        return lo, hi

    lane = lax.broadcasted_iota(jnp.int32, (1, LANES), 1) % HALF
    bases = (ctx * KEYS, far * KEYS)

    @pl.loop(0, CTX)
    def _(b):
        first = b * (2 * HALF) + half * HALF
        last = first + HALF - 1
        lo_all, full_hi = bounds(first)
        full_lo, hi_all = bounds(last)
        spans = []
        for base in bases:
            begin = jnp.clip(lo_all - base, 0, KEYS)
            end = jnp.clip(hi_all + 1 - base, 0, KEYS)
            spans.append((begin // TILE, jnp.where(end > begin, (end + TILE - 1) // TILE, begin // TILE)))
        some = (spans[0][1] > spans[0][0]) | (spans[1][1] > spans[1][0])

        @pl.when(jnp.logical_not(some))
        def _():
            ot_ref[b] = jnp.zeros((WIDTH, LANES), ot_ref.dtype)
            st_ref[b] = jnp.full((8, LANES), NEG, jnp.float32)

        @pl.when(some)
        def _():
            row_lo, row_hi = bounds(first + lane)
            for h in range(HEADS):
                wide = qg_ref[b, :, h * WIDTH : (h + 1) * WIDTH].astype(jnp.float32).T * SCALE
                high = wide.astype(jnp.bfloat16)
                qt_ref[:WIDTH, h * HALF : (h + 1) * HALF] = high
                qt_ref[WIDTH:, h * HALF : (h + 1) * HALF] = (wide - high.astype(jnp.float32)).astype(jnp.bfloat16)
            bad_ref[0] = jnp.int32(1)

            @pl.loop(0, 2)
            def _(attempt):
                @pl.when(bad_ref[0] == 1)
                def _():
                    m_ref[...] = jnp.full((8, LANES), LOW, jnp.float32)
                    acc_ref[...] = jnp.zeros_like(acc_ref)
                    bad_ref[1] = jnp.int32(0)

                    for part, (kr, base) in enumerate(zip((k_ref, ko_ref), bases)):

                        @pl.loop(spans[part][0], spans[part][1])
                        def _(t):
                            at = pl.multiple_of(t * TILE, TILE)
                            to = pl.multiple_of(part * KEYS + t * TILE, TILE)
                            begin = base + at
                            full = (begin >= full_lo) & (begin + TILE - 1 <= full_hi)
                            quick = full & (attempt == 0) & (bad_ref[1] == 1)

                            def scores(j):
                                kk = kr[pl.ds(at + j * SUB, SUB), :]
                                return jnp.dot(
                                    jnp.concatenate([kk, kk], axis=1), qt_ref[...], preferred_element_type=jnp.float32
                                )

                            def weigh(j, p):
                                return jnp.dot(
                                    vt_ref[:, pl.ds(to + j * SUB, SUB)],
                                    p.astype(jnp.bfloat16),
                                    preferred_element_type=jnp.float32,
                                )

                            @pl.when(quick)
                            def _():
                                m = m_ref[0:1, :]
                                total = acc_ref[...]
                                for j in range(TILE // SUB):
                                    total += weigh(j, jnp.exp2(scores(j) - m))
                                acc_ref[...] = total

                            @pl.when(jnp.logical_not(quick))
                            def _():
                                m_old = m_ref[0:1, :]
                                m = m_old
                                held = []
                                for j in range(TILE // SUB):
                                    s = scores(j)
                                    at_key = begin + j * SUB + lax.broadcasted_iota(jnp.int32, (SUB, LANES), 0)
                                    s = jnp.where((at_key >= row_lo) & (at_key <= row_hi), s, NEG)
                                    m = jnp.maximum(m, jnp.max(s, axis=0, keepdims=True))
                                    held.append(s)
                                total = acc_ref[...] * jnp.exp2(m_old - m)
                                for j in range(TILE // SUB):
                                    total += weigh(j, jnp.exp2(held[j] - m))
                                acc_ref[...] = total
                                m_ref[...] = jnp.broadcast_to(m, (8, LANES))
                                bad_ref[1] = jnp.int32(1)

                    fine = jnp.max(jnp.where(acc_ref[WIDTH : WIDTH + 8, :] < LARGE, 0.0, 1.0))
                    bad_ref[0] = jnp.where(fine > 0.0, 1, 0).astype(jnp.int32)

            total = acc_ref[WIDTH : WIDTH + 8, :]
            live = total > 0.0
            safe = jnp.where(live, total, 1.0)
            st_ref[b] = jnp.where(live, m_ref[...] + jnp.log2(safe), NEG)
            ot_ref[b] = (acc_ref[:WIDTH, :] * (1.0 / safe[0:1, :])).astype(ot_ref.dtype)


def attend(new_counts, prior_lengths, gathered, keys, values, far_keys, far_values):
    scalars = pl.BlockSpec(memory_space=pltpu.SMEM)
    vector = pl.BlockSpec(memory_space=pltpu.VMEM)
    return pl.pallas_call(
        attend_kernel,
        out_shape=(
            jax.ShapeDtypeStruct((CTX, WIDTH, LANES), jnp.bfloat16),
            jax.ShapeDtypeStruct((CTX, 8, LANES), jnp.float32),
        ),
        in_specs=[scalars] * 2 + [vector] * 5,
        out_specs=(vector, vector),
        scratch_shapes=[
            pltpu.VMEM((WIDTH + SUMS, 2 * KEYS), jnp.bfloat16),
            pltpu.VMEM((2 * WIDTH, LANES), jnp.bfloat16),
            pltpu.VMEM((8, LANES), jnp.float32),
            pltpu.VMEM((WIDTH + SUMS, LANES), jnp.float32),
            pltpu.SMEM((2,), jnp.int32),
        ],
        compiler_params=pltpu.CompilerParams(vmem_limit_bytes=VMEM),
        name="attend",
    )(new_counts, prior_lengths, gathered, keys, values, far_keys, far_values)


def combine_kernel(
    ot_ref, st_ref, att_ref, og_ref, sg_ref, own_sem, o_send, s_send, o_recv, s_recv, y_send, c_send, a_recv
):
    ctx, head = lax.axis_index("ctx"), lax.axis_index("head")
    y, core = head // 2, head % 2
    twin = y * 2 + (1 - core)

    def on_y(d):
        return lax.rem(y + d, SIDE) * 2 + core

    greet(
        [(lax.rem(ctx + d, CTX), head) for d in range(1, CTX)]
        + [(ctx, on_y(d)) for d in (1, 2, 3)]
        + [(ctx, twin)]
    )
    pending = []

    def start(copy):
        copy.start()
        pending.append(copy)

    for d in range(1, CTX):
        to = lax.rem(ctx + d, CTX)
        start(remote(st_ref.at[to], sg_ref.at[ctx], s_send.at[d], s_recv.at[ctx], to, head))
        start(remote(ot_ref.at[to], og_ref.at[ctx], o_send.at[d], o_recv.at[ctx], to, head))
    own = [
        pltpu.make_async_copy(ot_ref.at[ctx], og_ref.at[ctx], own_sem.at[0]),
        pltpu.make_async_copy(st_ref.at[ctx], sg_ref.at[ctx], own_sem.at[1]),
    ]
    for copy in own:
        copy.start()
    for copy in own:
        copy.wait()
    for d in range(1, CTX):
        of = lax.rem(ctx + d, CTX)
        remote(sg_ref.at[of], sg_ref.at[of], s_send.at[0], s_recv.at[of], ctx, head).wait_recv()
        remote(og_ref.at[of], og_ref.at[of], o_send.at[0], o_recv.at[of], ctx, head).wait_recv()

    def slot(p):
        return att_ref.at[:, pl.ds(pl.multiple_of(p * LANES, LANES), LANES)]

    mine = slot(head)
    for half in range(2):
        members = range(half * CTX // 2, (half + 1) * CTX // 2)
        top = sg_ref[members[0], 0:1, :]
        for i in members[1:]:
            top = jnp.maximum(top, sg_ref[i, 0:1, :])
        shares = [jnp.exp2(sg_ref[i, 0:1, :] - top) for i in members]
        inverse = 1.0 / functools.reduce(jnp.add, shares)
        out = jnp.zeros((WIDTH, LANES), jnp.float32)
        for i, share in zip(members, shares):
            out += og_ref[i].astype(jnp.float32) * (share * inverse)
        for h in range(HEADS):
            mine[half * HALF : (half + 1) * HALF, h * WIDTH : (h + 1) * WIDTH] = (
                out[:, h * HALF : (h + 1) * HALF].T.astype(att_ref.dtype)
            )

    for d in (1, 3, 2):
        start(remote(mine, mine, y_send.at[d - 1], a_recv.at[head], ctx, on_y(d)))
    start(remote(mine, mine, c_send.at[0], a_recv.at[head], ctx, twin))

    def arrived(p):
        remote(slot(p), slot(p), c_send.at[0], a_recv.at[p], ctx, head).wait_recv()

    for d in (1, 3, 2):
        p = on_y(d)
        arrived(p)
        start(remote(slot(p), slot(p), c_send.at[d], a_recv.at[p], ctx, twin))
    for d in range(SIDE):
        arrived(lax.rem(y + d, SIDE) * 2 + (1 - core))
    for copy in pending:
        copy.wait_send()


def combine(outs, logs):
    anywhere = pl.BlockSpec(memory_space=pl.ANY)
    dma = pltpu.SemaphoreType.DMA
    return pl.pallas_call(
        combine_kernel,
        out_shape=jax.ShapeDtypeStruct((2 * HALF, HEAD * LANES), outs.dtype),
        in_specs=[anywhere] * 2,
        out_specs=pl.BlockSpec(memory_space=pltpu.VMEM),
        scratch_shapes=[
            pltpu.VMEM(outs.shape, outs.dtype),
            pltpu.VMEM(logs.shape, logs.dtype),
            dma((2,)),
            dma((CTX,)),
            dma((CTX,)),
            dma((CTX,)),
            dma((CTX,)),
            dma((3,)),
            dma((SIDE,)),
            dma((HEAD,)),
        ],
        compiler_params=pltpu.CompilerParams(collective_id=1, has_side_effects=True, vmem_limit_bytes=VMEM),
        name="combine",
    )(outs, logs)


def body(queries, keys, values, w_out, new_counts, prior_lengths):
    gathered, far_keys, far_values = dispatch(queries, keys, values)
    outs, logs = attend(new_counts, prior_lengths, gathered, keys, values, far_keys, far_values)
    attended = combine(outs, logs)
    return jnp.dot(attended, w_out, preferred_element_type=jnp.float32).astype(jnp.bfloat16)


def solution(mesh):
    return jax.shard_map(
        body,
        mesh=mesh,
        in_specs=(P("ctx", "head"), P("ctx", None), P("ctx", None), P(None, "head"), P(), P()),
        out_specs=P("ctx", "head"),
        check_vma=False,
    )
```

```python
import functools
import math

import jax
import jax.numpy as jnp
from jax import lax
from jax.experimental import pallas as pl
from jax.experimental.pallas import tpu as pltpu
from jax.sharding import PartitionSpec as P

MESH = pl.DeviceIdType.MESH
CTX = 16
HEAD = 8
SIDE = 4
REQS = 8
HALF = 128
WIDTH = 128
HEADS = 2
LANES = HALF * HEADS
KEYS = 4096
PIECE = KEYS // HEAD
CHUNKS = 4
CHUNK = 2 * PIECE // CHUNKS
UNIT = 1024
ALIGN = 128
STEPS = CTX * (2 * KEYS // UNIT) + 4
LOW = -1e9
NEG = -1e30
SCALE = math.log2(math.e) / math.sqrt(WIDTH)
VMEM = 56 * 1024 * 1024


def remote(src, dst, send, recv, ctx, head):
    return pltpu.make_async_remote_copy(
        src_ref=src, dst_ref=dst, send_sem=send, recv_sem=recv, device_id=(ctx, head), device_id_type=MESH
    )


def greet(peers):
    barrier = pltpu.get_barrier_semaphore()
    for ctx, head in peers:
        pl.semaphore_signal(barrier, inc=1, device_id=(ctx, head), device_id_type=MESH)


def meet(peers):
    pl.semaphore_wait(pltpu.get_barrier_semaphore(), len(peers))


def dispatch_kernel(
    q_ref, k_ref, v_ref, qt_ref, kb_ref, vt_ref, qs_ref, vs_ref,
    own_sem, qz_send, qx_send, q_recv, kz_send, ky_send, kc_send, k_recv,
):
    ctx, head = lax.axis_index("ctx"), lax.axis_index("head")
    z, x = ctx // SIDE, ctx % SIDE
    y, core = head // 2, head % 2
    part = ctx // (CTX // 2)
    far = lax.rem(ctx + CTX // 2, CTX)
    twin = y * 2 + (1 - core)

    def zed(d):
        return lax.rem(z + d, SIDE)

    def on_x(d):
        return lax.rem(x + d, SIDE)

    def on_y(d):
        return lax.rem(y + d, SIDE) * 2 + core

    peers = (
        [(zed(d) * SIDE + x, head) for d in (1, 2, 3)]
        + [(z * SIDE + on_x(d), head) for d in (1, 3)]
        + [(ctx, on_y(d)) for d in (1, 3)]
        + [(ctx, twin)]
    )
    greet(peers)
    for rows in range(2):
        for h in range(HEADS):
            block = q_ref[rows * HALF : (rows + 1) * HALF, h * WIDTH : (h + 1) * WIDTH]
            qs_ref[rows, :, h * HALF : (h + 1) * HALF] = block.T

    @pl.loop(0, HEAD)
    def _(p):
        at = pl.multiple_of(p * PIECE, PIECE)
        vs_ref[:, pl.ds(at, PIECE)] = v_ref[pl.ds(at, PIECE), :].T

    meet(peers)
    pending = []

    def start(copy):
        copy.start()
        pending.append(copy)

    def head_offset(p, c):
        return p * PIECE + (c % 2) * CHUNK

    def source(c):
        at = pl.multiple_of(head_offset(head, c), CHUNK)
        return k_ref.at[pl.ds(at, CHUNK), :] if c < 2 else vs_ref.at[:, pl.ds(at, CHUNK)]

    def chunk(side, p, c):
        at = pl.multiple_of(side * KEYS + head_offset(p, c), CHUNK)
        return kb_ref.at[pl.ds(at, CHUNK), :] if c < 2 else vt_ref.at[:, pl.ds(at, CHUNK)]

    def share_q(slot, src, turn, ways):
        for d in ways:
            to = z * SIDE + on_x(d)
            start(remote(src, qt_ref.at[slot], qx_send.at[turn, d - 1], q_recv.at[slot], to, head))

    def arrived_q(slot):
        remote(qt_ref.at[slot], qt_ref.at[slot], qz_send.at[0], q_recv.at[slot], ctx, head).wait_recv()

    def pass_q(d):
        slot = zed(d) * SIDE + x
        arrived_q(slot)
        share_q(slot, qt_ref.at[slot], d, (1, 3))

    def relay_q(d):
        way = 1 if d in (0, 1) else 3
        slot = zed(d) * SIDE + on_x(4 - way)
        arrived_q(slot)
        to = z * SIDE + on_x(way)
        start(remote(qt_ref.at[slot], qt_ref.at[slot], qx_send.at[d, 1], q_recv.at[slot], to, head))

    def arrived_kv(p, c):
        ref = chunk(1 - part, p, c)
        remote(ref, ref, kz_send.at[0], k_recv.at[p, c], ctx, head).wait_recv()

    def send_kv(p, c, sem, to):
        ref = chunk(1 - part, p, c)
        start(remote(ref, ref, sem, k_recv.at[p, c], ctx, to))

    def pass_kv(c):
        arrived_kv(head, c)
        for d in (1, 3):
            send_kv(head, c, ky_send.at[c, d - 1], on_y(d))
        send_kv(head, c, kc_send.at[0, c], twin)

    def relay_kv(c):
        for d in (1, 3):
            p = on_y(d)
            arrived_kv(p, c)
            if (c % 2 == 0) == (d == 3):
                send_kv(p, c, ky_send.at[c, 1], on_y(4 - d))
            send_kv(p, c, kc_send.at[d, c], twin)

    def last_kv(c):
        p = on_y(2)
        arrived_kv(p, c)
        send_kv(p, c, kc_send.at[2, c], twin)

    for c in range(CHUNKS):
        start(remote(source(c), chunk(part, head, c), kz_send.at[c], k_recv.at[head, c], far, head))
        if c == 0:
            for d in (1, 3):
                zt = zed(d)
                start(remote(qs_ref.at[zt // 2], qt_ref.at[ctx], qz_send.at[d - 1], q_recv.at[ctx], zt * SIDE + x, head))
        if c == 1:
            zt = zed(2)
            start(remote(qs_ref.at[zt // 2], qt_ref.at[ctx], qz_send.at[1], q_recv.at[ctx], zt * SIDE + x, head))
    share_q(ctx, qs_ref.at[z // 2], 0, (1, 3))
    own = [
        pltpu.make_async_copy(qs_ref.at[z // 2], qt_ref.at[ctx], own_sem.at[0]),
        pltpu.make_async_copy(k_ref, kb_ref.at[pl.ds(pl.multiple_of(part * KEYS, KEYS), KEYS), :], own_sem.at[1]),
        pltpu.make_async_copy(vs_ref, vt_ref.at[:, pl.ds(pl.multiple_of(part * KEYS, KEYS), KEYS)], own_sem.at[2]),
    ]
    for copy in own:
        copy.start()

    pass_kv(0)
    pass_q(1)
    pass_q(3)
    relay_q(0)
    pass_kv(1)
    pass_q(2)
    relay_kv(0)
    pass_kv(2)
    relay_q(1)
    relay_q(3)
    relay_kv(1)
    pass_kv(3)
    relay_q(2)
    relay_kv(2)
    last_kv(0)
    relay_kv(3)
    last_kv(1)
    last_kv(2)
    last_kv(3)
    for d in range(SIDE):
        row = zed(d) * SIDE
        arrived_q(row + on_x(1 if d in (0, 1) else 3))
        arrived_q(row + on_x(2))
    for c in range(CHUNKS):
        for d in range(SIDE):
            arrived_kv(lax.rem(y + d, SIDE) * 2 + (1 - core), c)
    for copy in own:
        copy.wait()
    for copy in pending:
        copy.wait_send()


def dispatch(queries, keys, values):
    anywhere = pl.BlockSpec(memory_space=pl.ANY)
    vector = pl.BlockSpec(memory_space=pltpu.VMEM)
    dma = pltpu.SemaphoreType.DMA
    return pl.pallas_call(
        dispatch_kernel,
        out_shape=(
            jax.ShapeDtypeStruct((CTX, WIDTH, LANES), queries.dtype),
            jax.ShapeDtypeStruct((2 * KEYS, WIDTH), keys.dtype),
            jax.ShapeDtypeStruct((WIDTH, 2 * KEYS), values.dtype),
        ),
        in_specs=[vector, anywhere, vector],
        out_specs=(anywhere,) * 3,
        scratch_shapes=[
            pltpu.VMEM((2, WIDTH, LANES), queries.dtype),
            pltpu.VMEM((WIDTH, KEYS), values.dtype),
            dma((3,)),
            dma((3,)),
            dma((SIDE, 3)),
            dma((CTX,)),
            dma((CHUNKS,)),
            dma((CHUNKS, 3)),
            dma((SIDE, CHUNKS)),
            dma((HEAD, CHUNKS)),
        ],
        compiler_params=pltpu.CompilerParams(collective_id=0, has_side_effects=True, vmem_limit_bytes=VMEM),
        name="dispatch",
    )(queries, keys, values)


def attend_kernel(where_ref, new_ref, prior_ref, qt_any, k_any, vt_any, ot_ref, st_ref,
                  qt_ref, k_ref, vt_ref, s0_ref, s1_ref, x0_ref, x1_ref, m_ref, l_ref, acc_ref, tile_ref, pos_ref, mask_ref, load_sem):
    loads = [
        pltpu.make_async_copy(src, dst, load_sem.at[i])
        for i, (src, dst) in enumerate(((k_any, k_ref), (qt_any, qt_ref), (vt_any, vt_ref)))
    ]
    for load in loads:
        load.start()
    ctx = where_ref[0]
    half = ctx // (CTX // 2)
    base = lax.rem(ctx, CTX // 2) * KEYS

    q_start, k_start = [jnp.int32(0)], [jnp.int32(0)]
    for r in range(REQS - 1):
        q_start.append(q_start[-1] + new_ref[r])
        k_start.append(k_start[-1] + new_ref[r] + prior_ref[r])
    ahead = [prior_ref[r] + k_start[r] - q_start[r] for r in range(REQS)]
    lower = base
    upper = base + CTX // 2 * KEYS

    def bounds(row):
        lo, hi = jnp.zeros_like(row), jnp.full_like(row, ahead[0])
        for r in range(1, REQS):
            here = row >= q_start[r]
            lo = jnp.where(here, k_start[r], lo)
            hi = jnp.where(here, ahead[r], hi)
        return lo, row + hi

    def span(lo, hi):
        a0 = jnp.clip(lo - lower, 0, KEYS)
        e0 = jnp.clip(hi + 1 - lower, 0, KEYS)
        a1 = jnp.clip(lo - upper, 0, KEYS)
        e1 = jnp.clip(hi + 1 - upper, 0, KEYS)
        return jnp.where(e0 > a0, a0, KEYS + a1), jnp.where(e1 > a1, KEYS + e1, e0)

    def first_row(b):
        return b * (2 * HALF) + half * HALF

    def plan(b, count):
        lo_all, hi_one = bounds(first_row(b))
        lo_one, hi_all = bounds(first_row(b) + HALF - 1)
        begin, end = span(lo_all, hi_all)
        full_begin, full_end = span(lo_one, hi_one)
        full_end = jnp.where(hi_one >= lo_one, full_end, 0)
        begin = begin // ALIGN * ALIGN
        units = jnp.where(end > begin, (end - begin + UNIT - 1) // UNIT, 0)
        begin = jnp.minimum(begin, 2 * KEYS - UNIT * units)

        def put(u, _):
            at = begin + u * UNIT
            tile_ref[count + u] = b
            pos_ref[count + u] = at
            mask_ref[count + u] = jnp.where((at >= full_begin) & (at + UNIT <= full_end), 0, 1)
            return 0

        lax.fori_loop(0, units, put, 0)
        return count + units

    ot_ref[...] = jnp.zeros_like(ot_ref)
    st_ref[...] = jnp.full(st_ref.shape, NEG, jnp.float32)
    acc_ref[...] = jnp.zeros_like(acc_ref)
    l_ref[...] = jnp.zeros_like(l_ref)
    m_ref[...] = jnp.full_like(m_ref, LOW)
    lane = lax.broadcasted_iota(jnp.int32, (1, LANES), 1) % HALF
    count = lax.fori_loop(0, CTX, plan, jnp.int32(0))
    for i in range(3):
        tile_ref[count + i] = jnp.int32(CTX)
        pos_ref[count + i] = jnp.int32(0)
        mask_ref[count + i] = jnp.int32(0)

    def produce(i, s_ref, x_ref, masked):
        b = tile_ref[i]
        at = pl.multiple_of(pos_ref[i], ALIGN)
        s = jnp.dot(k_ref[pl.ds(at, UNIT), :], qt_ref[jnp.minimum(b, CTX - 1)], preferred_element_type=jnp.float32) * SCALE
        if masked:
            begin, end = span(*bounds(first_row(b) + lane))
            key = lax.broadcasted_iota(jnp.int32, (UNIT, LANES), 0)
            s = jnp.where((key >= begin - at) & (key < end - at), s, NEG)
        s_ref[...] = s
        x_ref[...] = jnp.max(s.reshape(UNIT // 8, 8, LANES), axis=0)

    def process(i, s_ref, x_ref):
        b = tile_ref[i]
        at = pl.multiple_of(pos_ref[i], ALIGN)
        first = tile_ref[jnp.maximum(i - 1, 0)] != b
        first = first | (i == 0)
        m_old = jnp.where(first, LOW, m_ref[0:1, :])
        m = jnp.maximum(m_old, jnp.max(x_ref[...], axis=0, keepdims=True))
        alpha = jnp.where(first, 0.0, jnp.exp2(m_old - m))
        p = jnp.exp2(s_ref[...] - m)
        m_ref[...] = jnp.broadcast_to(m, m_ref.shape)
        l_ref[...] = l_ref[...] * alpha + jnp.sum(p.reshape(UNIT // 8, 8, LANES), axis=0)
        acc_ref[...] = acc_ref[...] * alpha + jnp.dot(
            vt_ref[:, pl.ds(at, UNIT)], p.astype(jnp.bfloat16), preferred_element_type=jnp.float32
        )

    def finish(i):
        b = tile_ref[i]

        @pl.when((tile_ref[i + 1] != b) & (b < CTX))
        def _():
            total = jnp.sum(l_ref[...], axis=0, keepdims=True)
            live = total > 0.0
            safe = jnp.where(live, total, 1.0)
            st_ref[b] = jnp.broadcast_to(jnp.where(live, m_ref[0:1, :] + jnp.log2(safe), NEG), (8, LANES))
            ot_ref[b] = (acc_ref[...] * (1.0 / safe)).astype(ot_ref.dtype)

    def step(i, now, later):
        masked = mask_ref[i + 1] == 1

        @pl.when(masked)
        def _():
            produce(i + 1, *later, True)
            process(i, *now)

        @pl.when(jnp.logical_not(masked))
        def _():
            produce(i + 1, *later, False)
            process(i, *now)

        finish(i)

    even, odd = (s0_ref, x0_ref), (s1_ref, x1_ref)
    for load in loads:
        load.wait()
    produce(0, *even, True)

    @pl.loop(0, (count + 1) // 2)
    def _(i):
        step(2 * i, even, odd)
        step(2 * i + 1, odd, even)


def attend(where, new_counts, prior_lengths, gathered, keys, turned):
    scalars = pl.BlockSpec(memory_space=pltpu.SMEM)
    vector = pl.BlockSpec(memory_space=pltpu.VMEM)
    return pl.pallas_call(
        attend_kernel,
        out_shape=(
            jax.ShapeDtypeStruct((CTX, WIDTH, LANES), jnp.bfloat16),
            jax.ShapeDtypeStruct((CTX, 8, LANES), jnp.float32),
        ),
        in_specs=[scalars] * 3 + [pl.BlockSpec(memory_space=pl.ANY)] * 3,
        out_specs=(vector, vector),
        scratch_shapes=[
            pltpu.VMEM(gathered.shape, gathered.dtype),
            pltpu.VMEM(keys.shape, keys.dtype),
            pltpu.VMEM(turned.shape, turned.dtype),
            pltpu.VMEM((UNIT, LANES), jnp.float32),
            pltpu.VMEM((UNIT, LANES), jnp.float32),
            pltpu.VMEM((8, LANES), jnp.float32),
            pltpu.VMEM((8, LANES), jnp.float32),
            pltpu.VMEM((8, LANES), jnp.float32),
            pltpu.VMEM((8, LANES), jnp.float32),
            pltpu.VMEM((WIDTH, LANES), jnp.float32),
            pltpu.SMEM((STEPS,), jnp.int32),
            pltpu.SMEM((STEPS,), jnp.int32),
            pltpu.SMEM((STEPS,), jnp.int32),
            pltpu.SemaphoreType.DMA((3,)),
        ],
        compiler_params=pltpu.CompilerParams(vmem_limit_bytes=VMEM),
        name="attend",
    )(where, new_counts, prior_lengths, gathered, keys, turned)


def combine_kernel(
    ot_ref, st_ref, att_ref, og_ref, sg_ref, own_sem, o_send, s_send, o_recv, s_recv, y_send, c_send, a_recv
):
    ctx, head = lax.axis_index("ctx"), lax.axis_index("head")
    y, core = head // 2, head % 2
    twin = y * 2 + (1 - core)

    def on_y(d):
        return lax.rem(y + d, SIDE) * 2 + core

    peers = (
        [(lax.rem(ctx + d, CTX), head) for d in range(1, CTX)]
        + [(ctx, on_y(d)) for d in (1, 2, 3)]
        + [(ctx, twin)]
    )
    greet(peers)
    meet(peers)
    pending = []

    def start(copy):
        copy.start()
        pending.append(copy)

    for d in range(1, CTX):
        to = lax.rem(ctx + d, CTX)
        start(remote(st_ref.at[to], sg_ref.at[ctx], s_send.at[d], s_recv.at[ctx], to, head))
        start(remote(ot_ref.at[to], og_ref.at[ctx], o_send.at[d], o_recv.at[ctx], to, head))
    own = [
        pltpu.make_async_copy(ot_ref.at[ctx], og_ref.at[ctx], own_sem.at[0]),
        pltpu.make_async_copy(st_ref.at[ctx], sg_ref.at[ctx], own_sem.at[1]),
    ]
    for copy in own:
        copy.start()
    for copy in own:
        copy.wait()
    for d in range(1, CTX):
        of = lax.rem(ctx + d, CTX)
        remote(sg_ref.at[of], sg_ref.at[of], s_send.at[0], s_recv.at[of], ctx, head).wait_recv()
        remote(og_ref.at[of], og_ref.at[of], o_send.at[0], o_recv.at[of], ctx, head).wait_recv()

    def slot(p):
        return att_ref.at[:, pl.ds(pl.multiple_of(p * LANES, LANES), LANES)]

    mine = slot(head)
    for half in range(2):
        members = range(half * CTX // 2, (half + 1) * CTX // 2)
        top = sg_ref[members[0], 0:1, :]
        for i in members[1:]:
            top = jnp.maximum(top, sg_ref[i, 0:1, :])
        shares = [jnp.exp2(sg_ref[i, 0:1, :] - top) for i in members]
        inverse = 1.0 / functools.reduce(jnp.add, shares)
        out = jnp.zeros((WIDTH, LANES), jnp.float32)
        for i, share in zip(members, shares):
            out += og_ref[i].astype(jnp.float32) * (share * inverse)
        for h in range(HEADS):
            mine[half * HALF : (half + 1) * HALF, h * WIDTH : (h + 1) * WIDTH] = (
                out[:, h * HALF : (h + 1) * HALF].T.astype(att_ref.dtype)
            )

    for d in (1, 3, 2):
        start(remote(mine, mine, y_send.at[d - 1], a_recv.at[head], ctx, on_y(d)))
    start(remote(mine, mine, c_send.at[0], a_recv.at[head], ctx, twin))

    def arrived(p):
        remote(slot(p), slot(p), c_send.at[0], a_recv.at[p], ctx, head).wait_recv()

    for d in (1, 3, 2):
        p = on_y(d)
        arrived(p)
        start(remote(slot(p), slot(p), c_send.at[d], a_recv.at[p], ctx, twin))
    for d in range(SIDE):
        arrived(lax.rem(y + d, SIDE) * 2 + (1 - core))
    for copy in pending:
        copy.wait_send()


def combine(outs, logs):
    anywhere = pl.BlockSpec(memory_space=pl.ANY)
    dma = pltpu.SemaphoreType.DMA
    return pl.pallas_call(
        combine_kernel,
        out_shape=jax.ShapeDtypeStruct((2 * HALF, HEAD * LANES), outs.dtype),
        in_specs=[anywhere] * 2,
        out_specs=pl.BlockSpec(memory_space=pltpu.VMEM),
        scratch_shapes=[
            pltpu.VMEM(outs.shape, outs.dtype),
            pltpu.VMEM(logs.shape, logs.dtype),
            dma((2,)),
            dma((CTX,)),
            dma((CTX,)),
            dma((CTX,)),
            dma((CTX,)),
            dma((3,)),
            dma((SIDE,)),
            dma((HEAD,)),
        ],
        compiler_params=pltpu.CompilerParams(collective_id=1, has_side_effects=True, vmem_limit_bytes=VMEM),
        name="combine",
    )(outs, logs)


def body(queries, keys, values, w_out, new_counts, prior_lengths):
    where = lax.axis_index("ctx").astype(jnp.int32).reshape(1)
    gathered, cache, turned = dispatch(queries, keys, values)
    outs, logs = attend(where, new_counts, prior_lengths, gathered, cache, turned)
    attended = combine(outs, logs)
    return jnp.dot(attended, w_out, preferred_element_type=jnp.float32).astype(jnp.bfloat16)


def solution(mesh):
    return jax.shard_map(
        body,
        mesh=mesh,
        in_specs=(P("ctx", "head"), P("ctx", None), P("ctx", None), P(None, "head"), P(), P()),
        out_specs=P("ctx", "head"),
        check_vma=False,
    )
```

```python
import functools
import math

import jax
import jax.numpy as jnp
from jax import lax
from jax.experimental import pallas as pl
from jax.experimental.pallas import tpu as pltpu
from jax.sharding import PartitionSpec as P

MESH = pl.DeviceIdType.MESH
CTX = 16
HEAD = 8
SIDE = 4
REQS = 8
HALF = 128
WIDTH = 128
HEADS = 2
LANES = HALF * HEADS
KEYS = 4096
PIECE = KEYS // HEAD
CHUNKS = 4
CHUNK = 2 * PIECE // CHUNKS
COLUMNS = 512
FAR_FIRST = (
    (2, 2), (2, 1), (1, 2), (2, 3), (3, 2), (1, 1), (3, 3), (1, 3), (3, 1), (2, 0), (0, 2), (0, 1), (1, 0), (0, 3), (3, 0)
)
UNIT = 1024
ALIGN = CHUNK
STEPS = CTX * (2 * KEYS // UNIT) + 4
LOW = -1e9
NEG = -1e30
SCALE = math.log2(math.e) / math.sqrt(WIDTH)
VMEM = 56 * 1024 * 1024


def remote(src, dst, send, recv, ctx, head):
    return pltpu.make_async_remote_copy(
        src_ref=src, dst_ref=dst, send_sem=send, recv_sem=recv, device_id=(ctx, head), device_id_type=MESH
    )


def greet(peers):
    barrier = pltpu.get_barrier_semaphore()
    for ctx, head in peers:
        pl.semaphore_signal(barrier, inc=1, device_id=(ctx, head), device_id_type=MESH)


def meet(peers):
    pl.semaphore_wait(pltpu.get_barrier_semaphore(), len(peers))


def dispatch_kernel(
    q_ref, k_ref, v_ref, qt_ref, kf_ref, vf_ref, vo_ref, qs_ref, vs_ref,
    own_sem, qz_send, qx_send, q_recv, kz_send, ky_send, kc_send, k_recv,
):
    ctx, head = lax.axis_index("ctx"), lax.axis_index("head")
    z, x = ctx // SIDE, ctx % SIDE
    y, core = head // 2, head % 2
    far = lax.rem(ctx + CTX // 2, CTX)
    twin = y * 2 + (1 - core)

    def zed(d):
        return lax.rem(z + d, SIDE)

    def on_x(d):
        return lax.rem(x + d, SIDE)

    def on_y(d):
        return lax.rem(y + d, SIDE) * 2 + core

    peers = (
        [(zed(d) * SIDE + x, head) for d in (1, 2, 3)]
        + [(z * SIDE + on_x(d), head) for d in (1, 2, 3)]
        + [(ctx, on_y(d)) for d in (1, 2, 3)]
        + [(ctx, twin)]
    )
    greet(peers)
    for rows in range(2):
        for h in range(HEADS):
            block = q_ref[rows * HALF : (rows + 1) * HALF, h * WIDTH : (h + 1) * WIDTH]
            qs_ref[rows, :, h * HALF : (h + 1) * HALF] = block.T

    @pl.loop(0, KEYS // CHUNK)
    def _(p):
        vs_ref[p] = v_ref[pl.ds(pl.multiple_of(p * CHUNK, CHUNK), CHUNK), :].T

    meet(peers)
    pending = []

    def start(copy):
        copy.start()
        pending.append(copy)

    def number(p, c):
        return p * (PIECE // CHUNK) + c % 2

    def source(c):
        i = number(head, c)
        return k_ref.at[pl.ds(pl.multiple_of(i * CHUNK, CHUNK), CHUNK), :] if c < 2 else vs_ref.at[i]

    def chunk(p, c):
        i = number(p, c)
        return kf_ref.at[pl.ds(pl.multiple_of(i * CHUNK, CHUNK), CHUNK), :] if c < 2 else vf_ref.at[i]

    def share_q(slot, src, turn, ways):
        for d in ways:
            to = z * SIDE + on_x(d)
            start(remote(src, qt_ref.at[slot], qx_send.at[turn, d - 1], q_recv.at[slot], to, head))

    def arrived_q(slot):
        remote(qt_ref.at[slot], qt_ref.at[slot], qz_send.at[0], q_recv.at[slot], ctx, head).wait_recv()

    def pass_q(d):
        slot = zed(d) * SIDE + x
        arrived_q(slot)
        share_q(slot, qt_ref.at[slot], d, (1, 3, 2))

    def arrived_kv(p, c):
        ref = chunk(p, c)
        remote(ref, ref, kz_send.at[0], k_recv.at[p, c], ctx, head).wait_recv()

    def send_kv(p, c, sem, to):
        ref = chunk(p, c)
        start(remote(ref, ref, sem, k_recv.at[p, c], ctx, to))

    def pass_kv(c):
        arrived_kv(head, c)
        for d in (1, 3, 2):
            send_kv(head, c, ky_send.at[c, d - 1], on_y(d))
        send_kv(head, c, kc_send.at[0, c], twin)

    def relay_kv(c):
        for d in (1, 3):
            p = on_y(d)
            arrived_kv(p, c)
            send_kv(p, c, kc_send.at[d, c], twin)

    def last_kv(c):
        p = on_y(2)
        arrived_kv(p, c)
        send_kv(p, c, kc_send.at[2, c], twin)

    for c in range(CHUNKS):
        start(remote(source(c), chunk(head, c), kz_send.at[c], k_recv.at[head, c], far, head))
        if c == 0:
            for d in (1, 3):
                zt = zed(d)
                start(remote(qs_ref.at[zt // 2], qt_ref.at[ctx], qz_send.at[d - 1], q_recv.at[ctx], zt * SIDE + x, head))
        if c == 1:
            zt = zed(2)
            start(remote(qs_ref.at[zt // 2], qt_ref.at[ctx], qz_send.at[1], q_recv.at[ctx], zt * SIDE + x, head))
    share_q(ctx, qs_ref.at[z // 2], 0, (1, 3, 2))
    own = [
        pltpu.make_async_copy(qs_ref.at[z // 2], qt_ref.at[ctx], own_sem.at[0]),
        pltpu.make_async_copy(vs_ref, vo_ref, own_sem.at[1]),
    ]
    for copy in own:
        copy.start()

    pass_kv(0)
    pass_q(1)
    pass_q(3)
    pass_kv(1)
    pass_q(2)
    relay_kv(0)
    pass_kv(2)
    relay_kv(1)
    pass_kv(3)
    relay_kv(2)
    last_kv(0)
    relay_kv(3)
    last_kv(1)
    last_kv(2)
    last_kv(3)
    for d in range(SIDE):
        row = zed(d) * SIDE
        arrived_q(row + on_x(1))
        arrived_q(row + on_x(3))
        arrived_q(row + on_x(2))
    for c in range(CHUNKS):
        for d in range(SIDE):
            arrived_kv(lax.rem(y + d, SIDE) * 2 + (1 - core), c)
    for copy in own:
        copy.wait()
    for copy in pending:
        copy.wait_send()


def dispatch(queries, keys, values):
    anywhere = pl.BlockSpec(memory_space=pl.ANY)
    vector = pl.BlockSpec(memory_space=pltpu.VMEM)
    dma = pltpu.SemaphoreType.DMA
    return pl.pallas_call(
        dispatch_kernel,
        out_shape=(
            jax.ShapeDtypeStruct((CTX, WIDTH, LANES), queries.dtype),
            jax.ShapeDtypeStruct((KEYS, WIDTH), keys.dtype),
            jax.ShapeDtypeStruct((KEYS // CHUNK, WIDTH, CHUNK), values.dtype),
            jax.ShapeDtypeStruct((KEYS // CHUNK, WIDTH, CHUNK), values.dtype),
        ),
        in_specs=[vector, anywhere, vector],
        out_specs=(anywhere,) * 4,
        scratch_shapes=[
            pltpu.VMEM((2, WIDTH, LANES), queries.dtype),
            pltpu.VMEM((KEYS // CHUNK, WIDTH, CHUNK), values.dtype),
            dma((2,)),
            dma((3,)),
            dma((SIDE, 3)),
            dma((CTX,)),
            dma((CHUNKS,)),
            dma((CHUNKS, 3)),
            dma((SIDE, CHUNKS)),
            dma((HEAD, CHUNKS)),
        ],
        compiler_params=pltpu.CompilerParams(collective_id=0, has_side_effects=True, vmem_limit_bytes=VMEM),
        name="dispatch",
    )(queries, keys, values)


def attend_kernel(where_ref, new_ref, prior_ref, qt_any, k_any, kf_any, vo_any, vf_any, ot_ref, st_ref,
                  qt_ref, k_ref, vt_ref, s0_ref, s1_ref, x0_ref, x1_ref, m_ref, l_ref, acc_ref, tile_ref, pos_ref, mask_ref, load_sem):
    ctx = where_ref[0]
    half = ctx // (CTX // 2)
    mine, other = pl.multiple_of(half * KEYS, KEYS), pl.multiple_of((1 - half) * KEYS, KEYS)
    blocks = KEYS // CHUNK
    loads = [
        pltpu.make_async_copy(src, dst, load_sem.at[i])
        for i, (src, dst) in enumerate(
            (
                (qt_any, qt_ref),
                (k_any, k_ref.at[pl.ds(mine, KEYS), :]),
                (kf_any, k_ref.at[pl.ds(other, KEYS), :]),
                (vo_any, vt_ref.at[pl.ds(half * blocks, blocks)]),
                (vf_any, vt_ref.at[pl.ds((1 - half) * blocks, blocks)]),
            )
        )
    ]
    for load in loads:
        load.start()
    base = lax.rem(ctx, CTX // 2) * KEYS

    q_start, k_start = [jnp.int32(0)], [jnp.int32(0)]
    for r in range(REQS - 1):
        q_start.append(q_start[-1] + new_ref[r])
        k_start.append(k_start[-1] + new_ref[r] + prior_ref[r])
    ahead = [prior_ref[r] + k_start[r] - q_start[r] for r in range(REQS)]
    lower = base
    upper = base + CTX // 2 * KEYS

    def bounds(row):
        lo, hi = jnp.zeros_like(row), jnp.full_like(row, ahead[0])
        for r in range(1, REQS):
            here = row >= q_start[r]
            lo = jnp.where(here, k_start[r], lo)
            hi = jnp.where(here, ahead[r], hi)
        return lo, row + hi

    def span(lo, hi):
        a0 = jnp.clip(lo - lower, 0, KEYS)
        e0 = jnp.clip(hi + 1 - lower, 0, KEYS)
        a1 = jnp.clip(lo - upper, 0, KEYS)
        e1 = jnp.clip(hi + 1 - upper, 0, KEYS)
        return jnp.where(e0 > a0, a0, KEYS + a1), jnp.where(e1 > a1, KEYS + e1, e0)

    def first_row(b):
        return b * (2 * HALF) + half * HALF

    def plan(b, count):
        lo_all, hi_one = bounds(first_row(b))
        lo_one, hi_all = bounds(first_row(b) + HALF - 1)
        begin, end = span(lo_all, hi_all)
        full_begin, full_end = span(lo_one, hi_one)
        full_end = jnp.where(hi_one >= lo_one, full_end, 0)
        begin = begin // ALIGN * ALIGN
        units = jnp.where(end > begin, (end - begin + UNIT - 1) // UNIT, 0)
        begin = jnp.minimum(begin, 2 * KEYS - UNIT * units)

        def put(u, _):
            at = begin + u * UNIT
            tile_ref[count + u] = b
            pos_ref[count + u] = at
            mask_ref[count + u] = jnp.where((at >= full_begin) & (at + UNIT <= full_end), 0, 1)
            return 0

        lax.fori_loop(0, units, put, 0)
        return count + units

    ot_ref[...] = jnp.zeros_like(ot_ref)
    st_ref[...] = jnp.full(st_ref.shape, NEG, jnp.float32)
    acc_ref[...] = jnp.zeros_like(acc_ref)
    l_ref[...] = jnp.zeros_like(l_ref)
    m_ref[...] = jnp.full_like(m_ref, LOW)
    lane = lax.broadcasted_iota(jnp.int32, (1, LANES), 1) % HALF
    count = lax.fori_loop(0, CTX, plan, jnp.int32(0))
    for i in range(3):
        tile_ref[count + i] = jnp.int32(CTX)
        pos_ref[count + i] = jnp.int32(0)
        mask_ref[count + i] = jnp.int32(0)

    def produce(i, s_ref, x_ref, masked):
        b = tile_ref[i]
        at = pl.multiple_of(pos_ref[i], ALIGN)
        s = jnp.dot(k_ref[pl.ds(at, UNIT), :], qt_ref[jnp.minimum(b, CTX - 1)], preferred_element_type=jnp.float32) * SCALE
        if masked:
            begin, end = span(*bounds(first_row(b) + lane))
            key = lax.broadcasted_iota(jnp.int32, (UNIT, LANES), 0)
            s = jnp.where((key >= begin - at) & (key < end - at), s, NEG)
        s_ref[...] = s
        x_ref[...] = jnp.max(s.reshape(UNIT // 8, 8, LANES), axis=0)

    def process(i, s_ref, x_ref):
        b = tile_ref[i]
        at = pl.multiple_of(pos_ref[i], ALIGN)
        first = tile_ref[jnp.maximum(i - 1, 0)] != b
        first = first | (i == 0)
        m_old = jnp.where(first, LOW, m_ref[0:1, :])
        m = jnp.maximum(m_old, jnp.max(x_ref[...], axis=0, keepdims=True))
        alpha = jnp.where(first, 0.0, jnp.exp2(m_old - m))
        p = jnp.exp2(s_ref[...] - m)
        m_ref[...] = jnp.broadcast_to(m, m_ref.shape)
        l_ref[...] = l_ref[...] * alpha + jnp.sum(p.reshape(UNIT // 8, 8, LANES), axis=0)
        p = p.astype(jnp.bfloat16)
        total = acc_ref[...] * alpha
        for j in range(UNIT // CHUNK):
            total += jnp.dot(
                vt_ref[at // CHUNK + j], p[j * CHUNK : (j + 1) * CHUNK], preferred_element_type=jnp.float32
            )
        acc_ref[...] = total

    def finish(i):
        b = tile_ref[i]

        @pl.when((tile_ref[i + 1] != b) & (b < CTX))
        def _():
            total = jnp.sum(l_ref[...], axis=0, keepdims=True)
            live = total > 0.0
            safe = jnp.where(live, total, 1.0)
            log = jnp.where(live, m_ref[0:1, :] + jnp.log2(safe), NEG)
            out = (acc_ref[...] * (1.0 / safe)).astype(ot_ref.dtype)
            for h in range(HEADS):
                st_ref[b, h : h + 1, :] = log[:, h * HALF : (h + 1) * HALF]
                ot_ref[b, h] = out[:, h * HALF : (h + 1) * HALF]

    def step(i, now, later):
        masked = mask_ref[i + 1] == 1

        @pl.when(masked)
        def _():
            produce(i + 1, *later, True)
            process(i, *now)

        @pl.when(jnp.logical_not(masked))
        def _():
            produce(i + 1, *later, False)
            process(i, *now)

        finish(i)

    even, odd = (s0_ref, x0_ref), (s1_ref, x1_ref)
    for load in loads:
        load.wait()
    produce(0, *even, True)

    @pl.loop(0, (count + 1) // 2)
    def _(i):
        step(2 * i, even, odd)
        step(2 * i + 1, odd, even)


def attend(where, new_counts, prior_lengths, gathered, keys, far_keys, turned, far_turned):
    scalars = pl.BlockSpec(memory_space=pltpu.SMEM)
    vector = pl.BlockSpec(memory_space=pltpu.VMEM)
    return pl.pallas_call(
        attend_kernel,
        out_shape=(
            jax.ShapeDtypeStruct((CTX, HEADS, WIDTH, HALF), jnp.bfloat16),
            jax.ShapeDtypeStruct((CTX, 8, HALF), jnp.float32),
        ),
        in_specs=[scalars] * 3 + [pl.BlockSpec(memory_space=pl.ANY)] * 5,
        out_specs=(vector, vector),
        scratch_shapes=[
            pltpu.VMEM(gathered.shape, gathered.dtype),
            pltpu.VMEM((2 * KEYS, WIDTH), keys.dtype),
            pltpu.VMEM((2 * KEYS // CHUNK, WIDTH, CHUNK), turned.dtype),
            pltpu.VMEM((UNIT, LANES), jnp.float32),
            pltpu.VMEM((UNIT, LANES), jnp.float32),
            pltpu.VMEM((8, LANES), jnp.float32),
            pltpu.VMEM((8, LANES), jnp.float32),
            pltpu.VMEM((8, LANES), jnp.float32),
            pltpu.VMEM((8, LANES), jnp.float32),
            pltpu.VMEM((WIDTH, LANES), jnp.float32),
            pltpu.SMEM((STEPS,), jnp.int32),
            pltpu.SMEM((STEPS,), jnp.int32),
            pltpu.SMEM((STEPS,), jnp.int32),
            pltpu.SemaphoreType.DMA((5,)),
        ],
        compiler_params=pltpu.CompilerParams(vmem_limit_bytes=VMEM),
        name="attend",
    )(where, new_counts, prior_lengths, gathered, keys, far_keys, turned, far_turned)


def finish_kernel(
    ot_ref, st_ref, w_any, out_ref, og_ref, sg_ref, att_ref, w_ref, acc_ref,
    w_sem, own_sem, o_send, s_send, o_recv, s_recv, y_send, c_send, a_recv,
):
    ctx, head = lax.axis_index("ctx"), lax.axis_index("head")
    z, x = ctx // SIDE, ctx % SIDE
    y, core = head // 2, head % 2
    twin = y * 2 + (1 - core)

    def on_y(d):
        return lax.rem(y + d, SIDE) * 2 + core

    def at(steps):
        return lax.rem(z + steps[0], SIDE) * SIDE + lax.rem(x + steps[1], SIDE)

    peers = [(at(steps), head) for steps in FAR_FIRST] + [(ctx, on_y(d)) for d in (1, 2, 3)] + [(ctx, twin)]
    greet(peers)
    weights = pltpu.make_async_copy(w_any, w_ref, w_sem)
    weights.start()
    own = [pltpu.make_async_copy(st_ref.at[ctx], sg_ref.at[ctx], own_sem.at[0])]
    own += [pltpu.make_async_copy(ot_ref.at[ctx, h], og_ref.at[h, ctx], own_sem.at[1 + h]) for h in range(HEADS)]
    for copy in own:
        copy.start()
    meet(peers)
    pending = []

    def start(copy):
        copy.start()
        pending.append(copy)

    for i, steps in enumerate(FAR_FIRST):
        to = at(steps)
        start(remote(st_ref.at[to], sg_ref.at[ctx], s_send.at[i], s_recv.at[ctx], to, head))
        start(remote(ot_ref.at[to, 0], og_ref.at[0, ctx], o_send.at[0, i], o_recv.at[0, ctx], to, head))
    for h in range(1, HEADS):
        for i, steps in enumerate(FAR_FIRST):
            to = at(steps)
            start(remote(ot_ref.at[to, h], og_ref.at[h, ctx], o_send.at[h, i], o_recv.at[h, ctx], to, head))
    for copy in own:
        copy.wait()
    for steps in FAR_FIRST:
        of = at(steps)
        remote(sg_ref.at[of], sg_ref.at[of], s_send.at[0], s_recv.at[of], ctx, head).wait_recv()

    def arrived(h, p):
        ref = att_ref.at[h, p]
        remote(ref, ref, c_send.at[h, 0], a_recv.at[h, p], ctx, head).wait_recv()

    for h in range(HEADS):
        for steps in FAR_FIRST:
            of = at(steps)
            ref = og_ref.at[h, of]
            remote(ref, ref, o_send.at[h, 0], o_recv.at[h, of], ctx, head).wait_recv()
        for half in range(2):
            members = range(half * CTX // 2, (half + 1) * CTX // 2)
            logs = [sg_ref[i, h : h + 1, :] for i in members]
            top = functools.reduce(jnp.maximum, logs)
            shares = [jnp.exp2(log - top) for log in logs]
            inverse = 1.0 / functools.reduce(jnp.add, shares)
            out = jnp.zeros((WIDTH, HALF), jnp.float32)
            for i, share in zip(members, shares):
                out += og_ref[h, i].astype(jnp.float32) * (share * inverse)
            att_ref[h, head, half * HALF : (half + 1) * HALF, :] = out.T.astype(att_ref.dtype)
        mine = att_ref.at[h, head]
        for d in (2, 1, 3):
            start(remote(mine, mine, y_send.at[h, d - 1], a_recv.at[h, head], ctx, on_y(d)))
        start(remote(mine, mine, c_send.at[h, 0], a_recv.at[h, head], ctx, twin))
        for d in (1, 3, 2):
            p = on_y(d)
            arrived(h, p)
            ref = att_ref.at[h, p]
            start(remote(ref, ref, c_send.at[h, d], a_recv.at[h, p], ctx, twin))
        for d in range(SIDE):
            arrived(h, lax.rem(y + d, SIDE) * 2 + (1 - core))
        if h == 0:
            weights.wait()
        left = jnp.concatenate([att_ref[h, p] for p in range(HEAD)], axis=1)

        @pl.loop(0, w_ref.shape[2] // COLUMNS)
        def _(n):
            columns = pl.ds(pl.multiple_of(n * COLUMNS, COLUMNS), COLUMNS)
            right = jnp.concatenate([w_ref[HEADS * p + h, :, columns] for p in range(HEAD)], axis=0)
            product = jnp.dot(left, right, preferred_element_type=jnp.float32)
            if h == 0:
                acc_ref[:, columns] = product
            else:
                out_ref[:, columns] = (acc_ref[:, columns] + product).astype(out_ref.dtype)

    for copy in pending:
        copy.wait_send()


def finish(outs, logs, w_out):
    anywhere = pl.BlockSpec(memory_space=pl.ANY)
    dma = pltpu.SemaphoreType.DMA
    rows, width = 2 * HALF, w_out.shape[1]
    blocks = w_out.reshape(HEAD * HEADS, WIDTH, width)
    return pl.pallas_call(
        finish_kernel,
        out_shape=jax.ShapeDtypeStruct((rows, width), outs.dtype),
        in_specs=[anywhere] * 3,
        out_specs=pl.BlockSpec(memory_space=pltpu.VMEM),
        scratch_shapes=[
            pltpu.VMEM((HEADS, CTX, WIDTH, HALF), outs.dtype),
            pltpu.VMEM(logs.shape, logs.dtype),
            pltpu.VMEM((HEADS, HEAD, rows, WIDTH), outs.dtype),
            pltpu.VMEM(blocks.shape, blocks.dtype),
            pltpu.VMEM((rows, width), jnp.float32),
            dma,
            dma((1 + HEADS,)),
            dma((HEADS, CTX)),
            dma((CTX,)),
            dma((HEADS, CTX)),
            dma((CTX,)),
            dma((HEADS, 3)),
            dma((HEADS, SIDE)),
            dma((HEADS, HEAD)),
        ],
        compiler_params=pltpu.CompilerParams(collective_id=1, has_side_effects=True, vmem_limit_bytes=VMEM),
        name="finish",
    )(outs, logs, blocks)


def body(queries, keys, values, w_out, new_counts, prior_lengths):
    where = lax.axis_index("ctx").astype(jnp.int32).reshape(1)
    gathered, far_keys, far_turned, turned = dispatch(queries, keys, values)
    outs, logs = attend(where, new_counts, prior_lengths, gathered, keys, far_keys, turned, far_turned)
    return finish(outs, logs, w_out)


def solution(mesh):
    return jax.shard_map(
        body,
        mesh=mesh,
        in_specs=(P("ctx", "head"), P("ctx", None), P("ctx", None), P(None, "head"), P(), P()),
        out_specs=P("ctx", "head"),
        check_vma=False,
    )
```

```python
import functools
import math

import jax
import jax.numpy as jnp
from jax import lax
from jax.experimental import pallas as pl
from jax.experimental.pallas import tpu as pltpu
from jax.sharding import PartitionSpec as P

MESH = pl.DeviceIdType.MESH
CTX = 16
HEAD = 8
SIDE = 4
REQS = 8
HALF = 128
WIDTH = 128
HEADS = 2
LANES = HALF * HEADS
KEYS = 4096
PIECE = KEYS // HEAD
CHUNKS = 4
CHUNK = 2 * PIECE // CHUNKS
COLUMNS = 512
FAR_FIRST = (
    (2, 2), (2, 1), (1, 2), (2, 3), (3, 2), (1, 1), (3, 3), (1, 3), (3, 1), (2, 0), (0, 2), (0, 1), (1, 0), (0, 3), (3, 0)
)
UNIT = 2048
PART = 1024
ALIGN = CHUNK
STEPS = CTX * (2 * KEYS // PART + 1) + 4
LOW = -1e9
NEG = -1e30
SCALE = math.log2(math.e) / math.sqrt(WIDTH)
VMEM = 56 * 1024 * 1024


def remote(src, dst, send, recv, ctx, head):
    return pltpu.make_async_remote_copy(
        src_ref=src, dst_ref=dst, send_sem=send, recv_sem=recv, device_id=(ctx, head), device_id_type=MESH
    )


def greet(peers):
    barrier = pltpu.get_barrier_semaphore()
    for ctx, head in peers:
        pl.semaphore_signal(barrier, inc=1, device_id=(ctx, head), device_id_type=MESH)


def meet(peers):
    pl.semaphore_wait(pltpu.get_barrier_semaphore(), len(peers))


def dispatch_kernel(
    q_any, k_ref, v_any, qt_ref, kf_ref, vf_ref, vo_ref, q_ref, v_ref, qs_ref, vs_ref,
    own_sem, qz_send, qx_send, q_recv, kz_send, ky_send, kc_send, k_recv,
):
    ctx, head = lax.axis_index("ctx"), lax.axis_index("head")
    z, x = ctx // SIDE, ctx % SIDE
    y, core = head // 2, head % 2
    far = lax.rem(ctx + CTX // 2, CTX)
    twin = y * 2 + (1 - core)

    def zed(d):
        return lax.rem(z + d, SIDE)

    def on_x(d):
        return lax.rem(x + d, SIDE)

    def on_y(d):
        return lax.rem(y + d, SIDE) * 2 + core

    peers = (
        [(zed(d) * SIDE + x, head) for d in (1, 2, 3)]
        + [(z * SIDE + on_x(d), head) for d in (1, 2, 3)]
        + [(ctx, on_y(d)) for d in (1, 2, 3)]
        + [(ctx, twin)]
    )
    greet(peers)
    loads = [
        pltpu.make_async_copy(q_any, q_ref, own_sem.at[0]),
        pltpu.make_async_copy(v_any, v_ref, own_sem.at[1]),
    ]
    for load in loads:
        load.start()
    loads[0].wait()
    for rows in range(2):
        for h in range(HEADS):
            block = q_ref[rows * HALF : (rows + 1) * HALF, h * WIDTH : (h + 1) * WIDTH]
            qs_ref[rows, :, h * HALF : (h + 1) * HALF] = block.T

    loads[1].wait()

    @pl.loop(0, KEYS // CHUNK)
    def _(p):
        vs_ref[p] = v_ref[pl.ds(pl.multiple_of(p * CHUNK, CHUNK), CHUNK), :].T

    meet(peers)
    pending = []

    def start(copy):
        copy.start()
        pending.append(copy)

    def number(p, c):
        return p * (PIECE // CHUNK) + c % 2

    def source(c):
        i = number(head, c)
        return k_ref.at[pl.ds(pl.multiple_of(i * CHUNK, CHUNK), CHUNK), :] if c < 2 else vs_ref.at[i]

    def chunk(p, c):
        i = number(p, c)
        return kf_ref.at[pl.ds(pl.multiple_of(i * CHUNK, CHUNK), CHUNK), :] if c < 2 else vf_ref.at[i]

    def share_q(slot, src, turn, ways):
        for d in ways:
            to = z * SIDE + on_x(d)
            start(remote(src, qt_ref.at[slot], qx_send.at[turn, d - 1], q_recv.at[slot], to, head))

    def arrived_q(slot):
        remote(qt_ref.at[slot], qt_ref.at[slot], qz_send.at[0], q_recv.at[slot], ctx, head).wait_recv()

    def pass_q(d):
        slot = zed(d) * SIDE + x
        arrived_q(slot)
        share_q(slot, qt_ref.at[slot], d, (1, 3, 2))

    def arrived_kv(p, c):
        ref = chunk(p, c)
        remote(ref, ref, kz_send.at[0], k_recv.at[p, c], ctx, head).wait_recv()

    def send_kv(p, c, sem, to):
        ref = chunk(p, c)
        start(remote(ref, ref, sem, k_recv.at[p, c], ctx, to))

    def pass_kv(c):
        arrived_kv(head, c)
        for d in (1, 3, 2):
            send_kv(head, c, ky_send.at[c, d - 1], on_y(d))
        send_kv(head, c, kc_send.at[0, c], twin)

    def relay_kv(c):
        for d in (1, 3):
            p = on_y(d)
            arrived_kv(p, c)
            send_kv(p, c, kc_send.at[d, c], twin)

    def last_kv(c):
        p = on_y(2)
        arrived_kv(p, c)
        send_kv(p, c, kc_send.at[2, c], twin)

    for c in range(CHUNKS):
        start(remote(source(c), chunk(head, c), kz_send.at[c], k_recv.at[head, c], far, head))
        if c == 0:
            for d in (1, 3):
                zt = zed(d)
                start(remote(qs_ref.at[zt // 2], qt_ref.at[ctx], qz_send.at[d - 1], q_recv.at[ctx], zt * SIDE + x, head))
        if c == 1:
            zt = zed(2)
            start(remote(qs_ref.at[zt // 2], qt_ref.at[ctx], qz_send.at[1], q_recv.at[ctx], zt * SIDE + x, head))
    share_q(ctx, qs_ref.at[z // 2], 0, (1, 3, 2))
    own = [
        pltpu.make_async_copy(qs_ref.at[z // 2], qt_ref.at[ctx], own_sem.at[0]),
        pltpu.make_async_copy(vs_ref, vo_ref, own_sem.at[1]),
    ]
    for copy in own:
        copy.start()

    pass_kv(0)
    pass_q(1)
    pass_q(3)
    pass_kv(1)
    pass_q(2)
    relay_kv(0)
    pass_kv(2)
    relay_kv(1)
    pass_kv(3)
    relay_kv(2)
    last_kv(0)
    relay_kv(3)
    last_kv(1)
    last_kv(2)
    last_kv(3)
    for d in range(SIDE):
        row = zed(d) * SIDE
        arrived_q(row + on_x(1))
        arrived_q(row + on_x(3))
        arrived_q(row + on_x(2))
    for c in range(CHUNKS):
        for d in range(SIDE):
            arrived_kv(lax.rem(y + d, SIDE) * 2 + (1 - core), c)
    for copy in own:
        copy.wait()
    for copy in pending:
        copy.wait_send()


def dispatch(queries, keys, values):
    anywhere = pl.BlockSpec(memory_space=pl.ANY)
    held = pl.BlockSpec(memory_space=pltpu.HBM)
    dma = pltpu.SemaphoreType.DMA
    return pl.pallas_call(
        dispatch_kernel,
        out_shape=(
            jax.ShapeDtypeStruct((CTX, WIDTH, LANES), queries.dtype),
            jax.ShapeDtypeStruct((KEYS, WIDTH), keys.dtype),
            jax.ShapeDtypeStruct((KEYS // CHUNK, WIDTH, CHUNK), values.dtype),
            jax.ShapeDtypeStruct((KEYS // CHUNK, WIDTH, CHUNK), values.dtype),
        ),
        in_specs=[held] * 3,
        out_specs=(anywhere,) * 4,
        scratch_shapes=[
            pltpu.VMEM(queries.shape, queries.dtype),
            pltpu.VMEM(values.shape, values.dtype),
            pltpu.VMEM((2, WIDTH, LANES), queries.dtype),
            pltpu.VMEM((KEYS // CHUNK, WIDTH, CHUNK), values.dtype),
            dma((2,)),
            dma((3,)),
            dma((SIDE, 3)),
            dma((CTX,)),
            dma((CHUNKS,)),
            dma((CHUNKS, 3)),
            dma((SIDE, CHUNKS)),
            dma((HEAD, CHUNKS)),
        ],
        compiler_params=pltpu.CompilerParams(collective_id=0, has_side_effects=True, vmem_limit_bytes=48 * 1024 * 1024),
        name="dispatch",
    )(queries, keys, values)


def attend_kernel(where_ref, new_ref, prior_ref, qt_any, k_any, kf_any, vo_any, vf_any, ot_ref, st_ref,
                  qt_ref, k_ref, vt_ref, s0_ref, s1_ref, x0_ref, x1_ref, m_ref, l_ref, acc_ref, tile_ref, pos_ref, part_ref, load_sem):
    ctx = where_ref[0]
    half = ctx // (CTX // 2)
    mine, other = pl.multiple_of(half * KEYS, KEYS), pl.multiple_of((1 - half) * KEYS, KEYS)
    blocks = KEYS // CHUNK
    loads = [
        pltpu.make_async_copy(src, dst, load_sem.at[i])
        for i, (src, dst) in enumerate(
            (
                (qt_any, qt_ref),
                (k_any, k_ref.at[pl.ds(mine, KEYS), :]),
                (kf_any, k_ref.at[pl.ds(other, KEYS), :]),
                (vo_any, vt_ref.at[pl.ds(half * blocks, blocks)]),
                (vf_any, vt_ref.at[pl.ds((1 - half) * blocks, blocks)]),
            )
        )
    ]
    for load in loads:
        load.start()
    base = lax.rem(ctx, CTX // 2) * KEYS

    q_start, k_start = [jnp.int32(0)], [jnp.int32(0)]
    for r in range(REQS - 1):
        q_start.append(q_start[-1] + new_ref[r])
        k_start.append(k_start[-1] + new_ref[r] + prior_ref[r])
    ahead = [prior_ref[r] + k_start[r] - q_start[r] for r in range(REQS)]
    lower = base
    upper = base + CTX // 2 * KEYS

    def bounds(row):
        lo, hi = jnp.zeros_like(row), jnp.full_like(row, ahead[0])
        for r in range(1, REQS):
            here = row >= q_start[r]
            lo = jnp.where(here, k_start[r], lo)
            hi = jnp.where(here, ahead[r], hi)
        return lo, row + hi

    def span(lo, hi):
        a0 = jnp.clip(lo - lower, 0, KEYS)
        e0 = jnp.clip(hi + 1 - lower, 0, KEYS)
        a1 = jnp.clip(lo - upper, 0, KEYS)
        e1 = jnp.clip(hi + 1 - upper, 0, KEYS)
        return jnp.where(e0 > a0, a0, KEYS + a1), jnp.where(e1 > a1, KEYS + e1, e0)

    def first_row(b):
        return b * (2 * HALF) + half * HALF

    def plan(b, count):
        lo_all, hi_one = bounds(first_row(b))
        lo_one, hi_all = bounds(first_row(b) + HALF - 1)
        begin, end = span(lo_all, hi_all)
        full_begin, full_end = span(lo_one, hi_one)
        full_end = jnp.where(hi_one >= lo_one, full_end, 0)

        def put(state):
            at, i = state
            full = (at >= full_begin) & (at + UNIT <= full_end)
            tile_ref[i] = b
            pos_ref[i] = at
            part_ref[i] = jnp.where(full, 0, 1)
            return at + jnp.where(full, UNIT, PART), i + 1

        return lax.while_loop(lambda state: state[0] < end, put, (begin // ALIGN * ALIGN, count))[1]

    ot_ref[...] = jnp.zeros_like(ot_ref)
    st_ref[...] = jnp.full(st_ref.shape, NEG, jnp.float32)
    acc_ref[...] = jnp.zeros_like(acc_ref)
    vt_ref[2 * blocks :] = jnp.zeros((PART // CHUNK, WIDTH, CHUNK), vt_ref.dtype)
    l_ref[...] = jnp.zeros_like(l_ref)
    m_ref[...] = jnp.full_like(m_ref, LOW)
    lane = lax.broadcasted_iota(jnp.int32, (1, LANES), 1) % HALF
    count = lax.fori_loop(0, CTX, plan, jnp.int32(0))
    for i in range(3):
        tile_ref[count + i] = jnp.int32(CTX)
        pos_ref[count + i] = jnp.int32(0)
        part_ref[count + i] = jnp.int32(1)

    def produce(i, s_ref, x_ref, part):
        size = PART if part else UNIT
        b = tile_ref[i]
        at = pl.multiple_of(pos_ref[i], ALIGN)
        s = jnp.dot(k_ref[pl.ds(at, size), :], qt_ref[jnp.minimum(b, CTX - 1)], preferred_element_type=jnp.float32) * SCALE
        if part:
            begin, end = span(*bounds(first_row(b) + lane))
            key = lax.broadcasted_iota(jnp.int32, (size, LANES), 0)
            s = jnp.where((key >= begin - at) & (key < end - at), s, NEG)
        s_ref[:size, :] = s
        x_ref[...] = jnp.max(s.reshape(size // 8, 8, LANES), axis=0)

    def process(i, s_ref, x_ref, part):
        size = PART if part else UNIT
        b = tile_ref[i]
        at = pl.multiple_of(pos_ref[i], ALIGN)
        first = tile_ref[jnp.maximum(i - 1, 0)] != b
        first = first | (i == 0)
        m_old = jnp.where(first, LOW, m_ref[0:1, :])
        m = jnp.maximum(m_old, jnp.max(x_ref[...], axis=0, keepdims=True))
        alpha = jnp.where(first, 0.0, jnp.exp2(m_old - m))
        p = jnp.exp2(s_ref[:size, :] - m)
        m_ref[...] = jnp.broadcast_to(m, m_ref.shape)
        l_ref[...] = l_ref[...] * alpha + jnp.sum(p.reshape(size // 8, 8, LANES), axis=0)
        p = p.astype(jnp.bfloat16)
        total = acc_ref[...] * alpha
        for j in range(size // CHUNK):
            total += jnp.dot(
                vt_ref[at // CHUNK + j], p[j * CHUNK : (j + 1) * CHUNK], preferred_element_type=jnp.float32
            )
        acc_ref[...] = total

    def finish(i):
        b = tile_ref[i]

        @pl.when((tile_ref[i + 1] != b) & (b < CTX))
        def _():
            total = jnp.sum(l_ref[...], axis=0, keepdims=True)
            live = total > 0.0
            safe = jnp.where(live, total, 1.0)
            log = jnp.where(live, m_ref[0:1, :] + jnp.log2(safe), NEG)
            out = (acc_ref[...] * (1.0 / safe)).astype(ot_ref.dtype)
            for h in range(HEADS):
                st_ref[b, h : h + 1, :] = log[:, h * HALF : (h + 1) * HALF]
                ot_ref[b, h] = out[:, h * HALF : (h + 1) * HALF]

    def step(i, now, later):
        for after in range(2):
            for before in range(2):

                @pl.when((part_ref[i + 1] == after) & (part_ref[i] == before))
                def _():
                    produce(i + 1, *later, after)
                    process(i, *now, before)

        finish(i)

    even, odd = (s0_ref, x0_ref), (s1_ref, x1_ref)
    for load in loads:
        load.wait()
    for after in range(2):

        @pl.when(part_ref[0] == after)
        def _():
            produce(0, *even, after)

    @pl.loop(0, (count + 1) // 2)
    def _(i):
        step(2 * i, even, odd)
        step(2 * i + 1, odd, even)


def attend(where, new_counts, prior_lengths, gathered, keys, far_keys, turned, far_turned):
    scalars = pl.BlockSpec(memory_space=pltpu.SMEM)
    vector = pl.BlockSpec(memory_space=pltpu.VMEM)
    return pl.pallas_call(
        attend_kernel,
        out_shape=(
            jax.ShapeDtypeStruct((CTX, HEADS, WIDTH, HALF), jnp.bfloat16),
            jax.ShapeDtypeStruct((CTX, 8, HALF), jnp.float32),
        ),
        in_specs=[scalars] * 3 + [pl.BlockSpec(memory_space=pl.ANY), pl.BlockSpec(memory_space=pltpu.HBM)] + [pl.BlockSpec(memory_space=pl.ANY)] * 3,
        out_specs=(vector, vector),
        scratch_shapes=[
            pltpu.VMEM(gathered.shape, gathered.dtype),
            pltpu.VMEM((2 * KEYS + PART, WIDTH), keys.dtype),
            pltpu.VMEM(((2 * KEYS + PART) // CHUNK, WIDTH, CHUNK), turned.dtype),
            pltpu.VMEM((UNIT, LANES), jnp.float32),
            pltpu.VMEM((UNIT, LANES), jnp.float32),
            pltpu.VMEM((8, LANES), jnp.float32),
            pltpu.VMEM((8, LANES), jnp.float32),
            pltpu.VMEM((8, LANES), jnp.float32),
            pltpu.VMEM((8, LANES), jnp.float32),
            pltpu.VMEM((WIDTH, LANES), jnp.float32),
            pltpu.SMEM((STEPS,), jnp.int32),
            pltpu.SMEM((STEPS,), jnp.int32),
            pltpu.SMEM((STEPS,), jnp.int32),
            pltpu.SemaphoreType.DMA((5,)),
        ],
        compiler_params=pltpu.CompilerParams(vmem_limit_bytes=48 * 1024 * 1024),
        name="attend",
    )(where, new_counts, prior_lengths, gathered, keys, far_keys, turned, far_turned)


def finish_kernel(
    ot_ref, st_ref, w_any, out_ref, og_ref, sg_ref, att_ref, w_ref, acc_ref,
    w_sem, own_sem, o_send, s_send, o_recv, s_recv, y_send, c_send, a_recv,
):
    ctx, head = lax.axis_index("ctx"), lax.axis_index("head")
    z, x = ctx // SIDE, ctx % SIDE
    y, core = head // 2, head % 2
    twin = y * 2 + (1 - core)

    def on_y(d):
        return lax.rem(y + d, SIDE) * 2 + core

    def at(steps):
        return lax.rem(z + steps[0], SIDE) * SIDE + lax.rem(x + steps[1], SIDE)

    peers = [(at(steps), head) for steps in FAR_FIRST] + [(ctx, on_y(d)) for d in (1, 2, 3)] + [(ctx, twin)]
    greet(peers)
    weights = pltpu.make_async_copy(w_any, w_ref, w_sem)
    weights.start()
    own = [pltpu.make_async_copy(st_ref.at[ctx], sg_ref.at[ctx], own_sem.at[0])]
    own += [pltpu.make_async_copy(ot_ref.at[ctx, h], og_ref.at[h, ctx], own_sem.at[1 + h]) for h in range(HEADS)]
    for copy in own:
        copy.start()
    meet(peers)
    pending = []

    def start(copy):
        copy.start()
        pending.append(copy)

    for i, steps in enumerate(FAR_FIRST):
        to = at(steps)
        start(remote(st_ref.at[to], sg_ref.at[ctx], s_send.at[i], s_recv.at[ctx], to, head))
        start(remote(ot_ref.at[to, 0], og_ref.at[0, ctx], o_send.at[0, i], o_recv.at[0, ctx], to, head))
    for h in range(1, HEADS):
        for i, steps in enumerate(FAR_FIRST):
            to = at(steps)
            start(remote(ot_ref.at[to, h], og_ref.at[h, ctx], o_send.at[h, i], o_recv.at[h, ctx], to, head))
    for copy in own:
        copy.wait()
    for steps in FAR_FIRST:
        of = at(steps)
        remote(sg_ref.at[of], sg_ref.at[of], s_send.at[0], s_recv.at[of], ctx, head).wait_recv()

    def arrived(h, p):
        ref = att_ref.at[h, p]
        remote(ref, ref, c_send.at[h, 0], a_recv.at[h, p], ctx, head).wait_recv()

    for h in range(HEADS):
        for steps in FAR_FIRST:
            of = at(steps)
            ref = og_ref.at[h, of]
            remote(ref, ref, o_send.at[h, 0], o_recv.at[h, of], ctx, head).wait_recv()
        for half in range(2):
            members = range(half * CTX // 2, (half + 1) * CTX // 2)
            logs = [sg_ref[i, h : h + 1, :] for i in members]
            top = functools.reduce(jnp.maximum, logs)
            shares = [jnp.exp2(log - top) for log in logs]
            inverse = 1.0 / functools.reduce(jnp.add, shares)
            out = jnp.zeros((WIDTH, HALF), jnp.float32)
            for i, share in zip(members, shares):
                out += og_ref[h, i].astype(jnp.float32) * (share * inverse)
            att_ref[h, head, half * HALF : (half + 1) * HALF, :] = out.T.astype(att_ref.dtype)
        mine = att_ref.at[h, head]
        for d in (2, 1, 3):
            start(remote(mine, mine, y_send.at[h, d - 1], a_recv.at[h, head], ctx, on_y(d)))
        start(remote(mine, mine, c_send.at[h, 0], a_recv.at[h, head], ctx, twin))
        for d in (1, 3, 2):
            p = on_y(d)
            arrived(h, p)
            ref = att_ref.at[h, p]
            start(remote(ref, ref, c_send.at[h, d], a_recv.at[h, p], ctx, twin))
        for d in range(SIDE):
            arrived(h, lax.rem(y + d, SIDE) * 2 + (1 - core))
        if h == 0:
            weights.wait()
        left = jnp.concatenate([att_ref[h, p] for p in range(HEAD)], axis=1)

        @pl.loop(0, w_ref.shape[2] // COLUMNS)
        def _(n):
            columns = pl.ds(pl.multiple_of(n * COLUMNS, COLUMNS), COLUMNS)
            right = jnp.concatenate([w_ref[HEADS * p + h, :, columns] for p in range(HEAD)], axis=0)
            product = jnp.dot(left, right, preferred_element_type=jnp.float32)
            if h == 0:
                acc_ref[:, columns] = product
            else:
                out_ref[:, columns] = (acc_ref[:, columns] + product).astype(out_ref.dtype)

    for copy in pending:
        copy.wait_send()


def finish(outs, logs, w_out):
    anywhere = pl.BlockSpec(memory_space=pl.ANY)
    dma = pltpu.SemaphoreType.DMA
    rows, width = 2 * HALF, w_out.shape[1]
    blocks = pltpu.with_memory_space_constraint(w_out.reshape(HEAD * HEADS, WIDTH, width), pltpu.HBM)
    return pl.pallas_call(
        finish_kernel,
        out_shape=jax.ShapeDtypeStruct((rows, width), outs.dtype),
        in_specs=[anywhere, anywhere, pl.BlockSpec(memory_space=pltpu.HBM)],
        out_specs=pl.BlockSpec(memory_space=pltpu.VMEM),
        scratch_shapes=[
            pltpu.VMEM((HEADS, CTX, WIDTH, HALF), outs.dtype),
            pltpu.VMEM(logs.shape, logs.dtype),
            pltpu.VMEM((HEADS, HEAD, rows, WIDTH), outs.dtype),
            pltpu.VMEM(blocks.shape, blocks.dtype),
            pltpu.VMEM((rows, width), jnp.float32),
            dma,
            dma((1 + HEADS,)),
            dma((HEADS, CTX)),
            dma((CTX,)),
            dma((HEADS, CTX)),
            dma((CTX,)),
            dma((HEADS, 3)),
            dma((HEADS, SIDE)),
            dma((HEADS, HEAD)),
        ],
        compiler_params=pltpu.CompilerParams(collective_id=1, has_side_effects=True, vmem_limit_bytes=48 * 1024 * 1024),
        name="finish",
    )(outs, logs, blocks)


def body(*operands):
    w_out = operands[3]
    held = [pltpu.with_memory_space_constraint(array, pltpu.HBM) for array in operands if array is not w_out]
    queries, keys, values, new_counts, prior_lengths = held
    where = lax.axis_index("ctx").astype(jnp.int32).reshape(1)
    gathered, far_keys, far_turned, turned = dispatch(queries, keys, values)
    outs, logs = attend(where, new_counts, prior_lengths, gathered, keys, far_keys, turned, far_turned)
    return finish(outs, logs, w_out)


def solution(mesh):
    return jax.shard_map(
        body,
        mesh=mesh,
        in_specs=(P("ctx", "head"), P("ctx", None), P("ctx", None), P(None, "head"), P(), P()),
        out_specs=P("ctx", "head"),
        check_vma=False,
    )
```

```python
import functools
import math

import jax
import jax.numpy as jnp
from jax import lax
from jax.experimental import pallas as pl
from jax.experimental.pallas import tpu as pltpu
from jax.sharding import PartitionSpec as P

MESH = pl.DeviceIdType.MESH
CTX = 16
HEAD = 8
SIDE = 4
REQS = 8
HALF = 128
WIDTH = 128
HEADS = 2
LANES = HALF * HEADS
KEYS = 4096
PIECE = KEYS // HEAD
CHUNKS = 4
CHUNK = 2 * PIECE // CHUNKS
COLUMNS = 1024
FAR_FIRST = (
    (2, 2), (2, 1), (1, 2), (2, 3), (3, 2), (1, 1), (3, 3), (1, 3), (3, 1), (2, 0), (0, 2), (0, 1), (1, 0), (0, 3), (3, 0)
)
UNIT = 2048
PART = 1024
ALIGN = CHUNK
STEPS = CTX * (2 * KEYS // PART + 1) + 4
LOW = -1e9
NEG = -1e30
SCALE = math.log2(math.e) / math.sqrt(WIDTH)
VMEM = 56 * 1024 * 1024


def remote(src, dst, send, recv, ctx, head):
    return pltpu.make_async_remote_copy(
        src_ref=src, dst_ref=dst, send_sem=send, recv_sem=recv, device_id=(ctx, head), device_id_type=MESH
    )


def greet(peers):
    barrier = pltpu.get_barrier_semaphore()
    for ctx, head in peers:
        pl.semaphore_signal(barrier, inc=1, device_id=(ctx, head), device_id_type=MESH)


def meet(peers):
    pl.semaphore_wait(pltpu.get_barrier_semaphore(), len(peers))


def dispatch_kernel(
    q_any, k_ref, v_any, qt_ref, kf_ref, vf_ref, vo_ref, q_ref, v_ref, qs_ref, vs_ref,
    own_sem, qz_send, qx_send, q_recv, kz_send, ky_send, kc_send, k_recv,
):
    ctx, head = lax.axis_index("ctx"), lax.axis_index("head")
    z, x = ctx // SIDE, ctx % SIDE
    y, core = head // 2, head % 2
    far = lax.rem(ctx + CTX // 2, CTX)
    twin = y * 2 + (1 - core)

    def zed(d):
        return lax.rem(z + d, SIDE)

    def on_x(d):
        return lax.rem(x + d, SIDE)

    def on_y(d):
        return lax.rem(y + d, SIDE) * 2 + core

    peers = (
        [(zed(d) * SIDE + x, head) for d in (1, 2, 3)]
        + [(z * SIDE + on_x(d), head) for d in (1, 2, 3)]
        + [(ctx, on_y(d)) for d in (1, 2, 3)]
        + [(ctx, twin)]
    )
    greet(peers)
    loads = [
        pltpu.make_async_copy(q_any, q_ref, own_sem.at[0]),
        pltpu.make_async_copy(v_any, v_ref, own_sem.at[1]),
    ]
    for load in loads:
        load.start()
    loads[0].wait()
    for rows in range(2):
        for h in range(HEADS):
            block = q_ref[rows * HALF : (rows + 1) * HALF, h * WIDTH : (h + 1) * WIDTH]
            qs_ref[rows, :, h * HALF : (h + 1) * HALF] = block.T

    loads[1].wait()

    @pl.loop(0, KEYS // CHUNK)
    def _(p):
        vs_ref[p] = v_ref[pl.ds(pl.multiple_of(p * CHUNK, CHUNK), CHUNK), :].T

    meet(peers)
    pending = []

    def start(copy):
        copy.start()
        pending.append(copy)

    def number(p, c):
        return p * (PIECE // CHUNK) + c % 2

    def source(c):
        i = number(head, c)
        return k_ref.at[pl.ds(pl.multiple_of(i * CHUNK, CHUNK), CHUNK), :] if c < 2 else vs_ref.at[i]

    def chunk(p, c):
        i = number(p, c)
        return kf_ref.at[pl.ds(pl.multiple_of(i * CHUNK, CHUNK), CHUNK), :] if c < 2 else vf_ref.at[i]

    def share_q(slot, src, turn, ways):
        for d in ways:
            to = z * SIDE + on_x(d)
            start(remote(src, qt_ref.at[slot], qx_send.at[turn, d - 1], q_recv.at[slot], to, head))

    def arrived_q(slot):
        remote(qt_ref.at[slot], qt_ref.at[slot], qz_send.at[0], q_recv.at[slot], ctx, head).wait_recv()

    def pass_q(d):
        slot = zed(d) * SIDE + x
        arrived_q(slot)
        share_q(slot, qt_ref.at[slot], d, (1, 3, 2))

    def arrived_kv(p, c):
        ref = chunk(p, c)
        remote(ref, ref, kz_send.at[0], k_recv.at[p, c], ctx, head).wait_recv()

    def send_kv(p, c, sem, to):
        ref = chunk(p, c)
        start(remote(ref, ref, sem, k_recv.at[p, c], ctx, to))

    def pass_kv(c):
        arrived_kv(head, c)
        for d in (1, 3, 2):
            send_kv(head, c, ky_send.at[c, d - 1], on_y(d))
        send_kv(head, c, kc_send.at[0, c], twin)

    def relay_kv(c):
        for d in (1, 3):
            p = on_y(d)
            arrived_kv(p, c)
            send_kv(p, c, kc_send.at[d, c], twin)

    def last_kv(c):
        p = on_y(2)
        arrived_kv(p, c)
        send_kv(p, c, kc_send.at[2, c], twin)

    for c in range(CHUNKS):
        start(remote(source(c), chunk(head, c), kz_send.at[c], k_recv.at[head, c], far, head))
        if c == 0:
            for d in (1, 3):
                zt = zed(d)
                start(remote(qs_ref.at[zt // 2], qt_ref.at[ctx], qz_send.at[d - 1], q_recv.at[ctx], zt * SIDE + x, head))
        if c == 1:
            zt = zed(2)
            start(remote(qs_ref.at[zt // 2], qt_ref.at[ctx], qz_send.at[1], q_recv.at[ctx], zt * SIDE + x, head))
    share_q(ctx, qs_ref.at[z // 2], 0, (1, 3, 2))
    own = [
        pltpu.make_async_copy(qs_ref.at[z // 2], qt_ref.at[ctx], own_sem.at[0]),
        pltpu.make_async_copy(vs_ref, vo_ref, own_sem.at[1]),
    ]
    for copy in own:
        copy.start()

    pass_kv(0)
    pass_q(1)
    pass_q(3)
    pass_kv(1)
    pass_q(2)
    relay_kv(0)
    pass_kv(2)
    relay_kv(1)
    pass_kv(3)
    relay_kv(2)
    last_kv(0)
    relay_kv(3)
    last_kv(1)
    last_kv(2)
    last_kv(3)
    for d in range(SIDE):
        row = zed(d) * SIDE
        arrived_q(row + on_x(1))
        arrived_q(row + on_x(3))
        arrived_q(row + on_x(2))
    for c in range(CHUNKS):
        for d in range(SIDE):
            arrived_kv(lax.rem(y + d, SIDE) * 2 + (1 - core), c)
    for copy in own:
        copy.wait()
    for copy in pending:
        copy.wait_send()


def dispatch(queries, keys, values):
    anywhere = pl.BlockSpec(memory_space=pl.ANY)
    held = pl.BlockSpec(memory_space=pltpu.HBM)
    dma = pltpu.SemaphoreType.DMA
    return pl.pallas_call(
        dispatch_kernel,
        out_shape=(
            jax.ShapeDtypeStruct((CTX, WIDTH, LANES), queries.dtype),
            jax.ShapeDtypeStruct((KEYS, WIDTH), keys.dtype),
            jax.ShapeDtypeStruct((KEYS // CHUNK, WIDTH, CHUNK), values.dtype),
            jax.ShapeDtypeStruct((KEYS // CHUNK, WIDTH, CHUNK), values.dtype),
        ),
        in_specs=[held] * 3,
        out_specs=(anywhere,) * 4,
        scratch_shapes=[
            pltpu.VMEM(queries.shape, queries.dtype),
            pltpu.VMEM(values.shape, values.dtype),
            pltpu.VMEM((2, WIDTH, LANES), queries.dtype),
            pltpu.VMEM((KEYS // CHUNK, WIDTH, CHUNK), values.dtype),
            dma((2,)),
            dma((3,)),
            dma((SIDE, 3)),
            dma((CTX,)),
            dma((CHUNKS,)),
            dma((CHUNKS, 3)),
            dma((SIDE, CHUNKS)),
            dma((HEAD, CHUNKS)),
        ],
        compiler_params=pltpu.CompilerParams(collective_id=0, has_side_effects=True, vmem_limit_bytes=48 * 1024 * 1024),
        name="dispatch",
    )(queries, keys, values)


def attend_kernel(where_ref, new_ref, prior_ref, qt_any, k_any, kf_any, vo_any, vf_any, ot_ref, st_ref,
                  qt_ref, k_ref, vt_ref, s0_ref, s1_ref, x0_ref, x1_ref, m_ref, l_ref, acc_ref, tile_ref, pos_ref, part_ref, load_sem):
    ctx = where_ref[0]
    half = ctx // (CTX // 2)
    mine, other = pl.multiple_of(half * KEYS, KEYS), pl.multiple_of((1 - half) * KEYS, KEYS)
    blocks = KEYS // CHUNK
    loads = [
        pltpu.make_async_copy(src, dst, load_sem.at[i])
        for i, (src, dst) in enumerate(
            (
                (qt_any, qt_ref),
                (k_any, k_ref.at[pl.ds(mine, KEYS), :]),
                (kf_any, k_ref.at[pl.ds(other, KEYS), :]),
                (vo_any, vt_ref.at[pl.ds(half * blocks, blocks)]),
                (vf_any, vt_ref.at[pl.ds((1 - half) * blocks, blocks)]),
            )
        )
    ]
    for load in loads:
        load.start()
    base = lax.rem(ctx, CTX // 2) * KEYS

    q_start, k_start = [jnp.int32(0)], [jnp.int32(0)]
    for r in range(REQS - 1):
        q_start.append(q_start[-1] + new_ref[r])
        k_start.append(k_start[-1] + new_ref[r] + prior_ref[r])
    ahead = [prior_ref[r] + k_start[r] - q_start[r] for r in range(REQS)]
    lower = base
    upper = base + CTX // 2 * KEYS

    def bounds(row):
        lo, hi = jnp.zeros_like(row), jnp.full_like(row, ahead[0])
        for r in range(1, REQS):
            here = row >= q_start[r]
            lo = jnp.where(here, k_start[r], lo)
            hi = jnp.where(here, ahead[r], hi)
        return lo, row + hi

    def span(lo, hi):
        a0 = jnp.clip(lo - lower, 0, KEYS)
        e0 = jnp.clip(hi + 1 - lower, 0, KEYS)
        a1 = jnp.clip(lo - upper, 0, KEYS)
        e1 = jnp.clip(hi + 1 - upper, 0, KEYS)
        return jnp.where(e0 > a0, a0, KEYS + a1), jnp.where(e1 > a1, KEYS + e1, e0)

    def first_row(b):
        return b * (2 * HALF) + half * HALF

    def plan(b, count):
        lo_all, hi_one = bounds(first_row(b))
        lo_one, hi_all = bounds(first_row(b) + HALF - 1)
        begin, end = span(lo_all, hi_all)
        full_begin, full_end = span(lo_one, hi_one)
        full_end = jnp.where(hi_one >= lo_one, full_end, 0)

        def put(state):
            at, i = state
            full = (at >= full_begin) & (at + UNIT <= full_end)
            tile_ref[i] = b
            pos_ref[i] = at
            part_ref[i] = jnp.where(full, 0, 1)
            return at + jnp.where(full, UNIT, PART), i + 1

        return lax.while_loop(lambda state: state[0] < end, put, (begin // ALIGN * ALIGN, count))[1]

    ot_ref[...] = jnp.zeros_like(ot_ref)
    st_ref[...] = jnp.full(st_ref.shape, NEG, jnp.float32)
    acc_ref[...] = jnp.zeros_like(acc_ref)
    vt_ref[2 * blocks :] = jnp.zeros((PART // CHUNK, WIDTH, CHUNK), vt_ref.dtype)
    l_ref[...] = jnp.zeros_like(l_ref)
    m_ref[...] = jnp.full_like(m_ref, LOW)
    lane = lax.broadcasted_iota(jnp.int32, (1, LANES), 1) % HALF
    count = lax.fori_loop(0, CTX, plan, jnp.int32(0))
    for i in range(3):
        tile_ref[count + i] = jnp.int32(CTX)
        pos_ref[count + i] = jnp.int32(0)
        part_ref[count + i] = jnp.int32(1)

    def produce(i, s_ref, x_ref, part):
        size = PART if part else UNIT
        b = tile_ref[i]
        at = pl.multiple_of(pos_ref[i], ALIGN)
        s = jnp.dot(k_ref[pl.ds(at, size), :], qt_ref[jnp.minimum(b, CTX - 1)], preferred_element_type=jnp.float32) * SCALE
        if part:
            begin, end = span(*bounds(first_row(b) + lane))
            key = lax.broadcasted_iota(jnp.int32, (size, LANES), 0)
            s = jnp.where((key >= begin - at) & (key < end - at), s, NEG)
        s_ref[:size, :] = s
        x_ref[...] = jnp.max(s.reshape(size // 8, 8, LANES), axis=0)

    def process(i, s_ref, x_ref, part):
        size = PART if part else UNIT
        b = tile_ref[i]
        at = pl.multiple_of(pos_ref[i], ALIGN)
        first = tile_ref[jnp.maximum(i - 1, 0)] != b
        first = first | (i == 0)
        m_old = jnp.where(first, LOW, m_ref[0:1, :])
        m = jnp.maximum(m_old, jnp.max(x_ref[...], axis=0, keepdims=True))
        alpha = jnp.where(first, 0.0, jnp.exp2(m_old - m))
        p = jnp.exp2(s_ref[:size, :] - m)
        m_ref[...] = jnp.broadcast_to(m, m_ref.shape)
        l_ref[...] = l_ref[...] * alpha + jnp.sum(p.reshape(size // 8, 8, LANES), axis=0)
        p = p.astype(jnp.bfloat16)
        total = acc_ref[...] * alpha
        for j in range(size // CHUNK):
            total += jnp.dot(
                vt_ref[at // CHUNK + j], p[j * CHUNK : (j + 1) * CHUNK], preferred_element_type=jnp.float32
            )
        acc_ref[...] = total

    def finish(i):
        b = tile_ref[i]

        @pl.when((tile_ref[i + 1] != b) & (b < CTX))
        def _():
            total = jnp.sum(l_ref[...], axis=0, keepdims=True)
            live = total > 0.0
            safe = jnp.where(live, total, 1.0)
            log = jnp.where(live, m_ref[0:1, :] + jnp.log2(safe), NEG)
            out = (acc_ref[...] * (1.0 / safe)).astype(ot_ref.dtype)
            for h in range(HEADS):
                st_ref[b, h : h + 1, :] = log[:, h * HALF : (h + 1) * HALF]
                ot_ref[b, h] = out[:, h * HALF : (h + 1) * HALF]

    def step(i, now, later):
        for after in range(2):
            for before in range(2):

                @pl.when((part_ref[i + 1] == after) & (part_ref[i] == before))
                def _():
                    produce(i + 1, *later, after)
                    process(i, *now, before)

        finish(i)

    even, odd = (s0_ref, x0_ref), (s1_ref, x1_ref)
    for load in loads:
        load.wait()
    for after in range(2):

        @pl.when(part_ref[0] == after)
        def _():
            produce(0, *even, after)

    @pl.loop(0, (count + 1) // 2)
    def _(i):
        step(2 * i, even, odd)
        step(2 * i + 1, odd, even)


def attend(where, new_counts, prior_lengths, gathered, keys, far_keys, turned, far_turned):
    scalars = pl.BlockSpec(memory_space=pltpu.SMEM)
    vector = pl.BlockSpec(memory_space=pltpu.VMEM)
    return pl.pallas_call(
        attend_kernel,
        out_shape=(
            jax.ShapeDtypeStruct((CTX, HEADS, WIDTH, HALF), jnp.bfloat16),
            jax.ShapeDtypeStruct((CTX, 8, HALF), jnp.float32),
        ),
        in_specs=[scalars] * 3 + [pl.BlockSpec(memory_space=pl.ANY), pl.BlockSpec(memory_space=pltpu.HBM)] + [pl.BlockSpec(memory_space=pl.ANY)] * 3,
        out_specs=(vector, vector),
        scratch_shapes=[
            pltpu.VMEM(gathered.shape, gathered.dtype),
            pltpu.VMEM((2 * KEYS + PART, WIDTH), keys.dtype),
            pltpu.VMEM(((2 * KEYS + PART) // CHUNK, WIDTH, CHUNK), turned.dtype),
            pltpu.VMEM((UNIT, LANES), jnp.float32),
            pltpu.VMEM((UNIT, LANES), jnp.float32),
            pltpu.VMEM((8, LANES), jnp.float32),
            pltpu.VMEM((8, LANES), jnp.float32),
            pltpu.VMEM((8, LANES), jnp.float32),
            pltpu.VMEM((8, LANES), jnp.float32),
            pltpu.VMEM((WIDTH, LANES), jnp.float32),
            pltpu.SMEM((STEPS,), jnp.int32),
            pltpu.SMEM((STEPS,), jnp.int32),
            pltpu.SMEM((STEPS,), jnp.int32),
            pltpu.SemaphoreType.DMA((5,)),
        ],
        compiler_params=pltpu.CompilerParams(vmem_limit_bytes=48 * 1024 * 1024),
        name="attend",
    )(where, new_counts, prior_lengths, gathered, keys, far_keys, turned, far_turned)


def finish_kernel(
    ot_ref, st_ref, w_any, out_ref, og_ref, sg_ref, att_ref, w_ref, acc_ref,
    w_sem, own_sem, o_send, s_send, o_recv, s_recv, y_send, c_send, a_recv,
):
    ctx, head = lax.axis_index("ctx"), lax.axis_index("head")
    z, x = ctx // SIDE, ctx % SIDE
    y, core = head // 2, head % 2
    twin = y * 2 + (1 - core)

    def on_y(d):
        return lax.rem(y + d, SIDE) * 2 + core

    def at(steps):
        return lax.rem(z + steps[0], SIDE) * SIDE + lax.rem(x + steps[1], SIDE)

    peers = [(at(steps), head) for steps in FAR_FIRST] + [(ctx, on_y(d)) for d in (1, 2, 3)] + [(ctx, twin)]
    greet(peers)
    weights = pltpu.make_async_copy(w_any, w_ref, w_sem)
    weights.start()
    own = [pltpu.make_async_copy(st_ref.at[ctx], sg_ref.at[ctx], own_sem.at[0])]
    own += [pltpu.make_async_copy(ot_ref.at[ctx, h], og_ref.at[h, ctx], own_sem.at[1 + h]) for h in range(HEADS)]
    for copy in own:
        copy.start()
    meet(peers)
    pending = []

    def start(copy):
        copy.start()
        pending.append(copy)

    for i, steps in enumerate(FAR_FIRST):
        to = at(steps)
        start(remote(st_ref.at[to], sg_ref.at[ctx], s_send.at[i], s_recv.at[ctx], to, head))
        start(remote(ot_ref.at[to, 0], og_ref.at[0, ctx], o_send.at[0, i], o_recv.at[0, ctx], to, head))
    for h in range(1, HEADS):
        for i, steps in enumerate(FAR_FIRST):
            to = at(steps)
            start(remote(ot_ref.at[to, h], og_ref.at[h, ctx], o_send.at[h, i], o_recv.at[h, ctx], to, head))
    for copy in own:
        copy.wait()
    for steps in FAR_FIRST:
        of = at(steps)
        remote(sg_ref.at[of], sg_ref.at[of], s_send.at[0], s_recv.at[of], ctx, head).wait_recv()

    def share(h, p, r):
        return att_ref.at[h, p, pl.ds(r * HALF, HALF), :]

    def arrived(h, p, r):
        ref = share(h, p, r)
        remote(ref, ref, c_send.at[h, r, 0], a_recv.at[h, p, r], ctx, head).wait_recv()

    def send(h, p, r, sem, to):
        ref = share(h, p, r)
        start(remote(ref, ref, sem, a_recv.at[h, p, r], ctx, to))

    def merge(h):
        for steps in FAR_FIRST:
            of = at(steps)
            ref = og_ref.at[h, of]
            remote(ref, ref, o_send.at[h, 0], o_recv.at[h, of], ctx, head).wait_recv()
        for half in range(2):
            members = range(half * CTX // 2, (half + 1) * CTX // 2)
            logs = [sg_ref[i, h : h + 1, :] for i in members]
            top = functools.reduce(jnp.maximum, logs)
            shares = [jnp.exp2(log - top) for log in logs]
            inverse = 1.0 / functools.reduce(jnp.add, shares)
            out = jnp.zeros((WIDTH, HALF), jnp.float32)
            for i, part in zip(members, shares):
                out += og_ref[h, i].astype(jnp.float32) * (part * inverse)
            att_ref[h, head, half * HALF : (half + 1) * HALF, :] = out.T.astype(att_ref.dtype)
            for d in (2, 1, 3):
                send(h, head, half, y_send.at[h, half, d - 1], on_y(d))
            send(h, head, half, c_send.at[h, half, 0], twin)

    def forward(h):
        for r in range(2):
            for d in (1, 3, 2):
                p = on_y(d)
                arrived(h, p, r)
                send(h, p, r, c_send.at[h, r, d], twin)

    def gathered(h):
        for r in range(2):
            for d in range(SIDE):
                arrived(h, lax.rem(y + d, SIDE) * 2 + (1 - core), r)

    def multiply(h, side, begin, end):
        pieces = [lax.rem(y + d, SIDE) * 2 + side for d in range(SIDE)]
        left = jnp.concatenate([att_ref[h, p] for p in pieces], axis=1)

        @pl.loop(0, w_ref.shape[2] // COLUMNS)
        def _(n):
            columns = pl.ds(pl.multiple_of(n * COLUMNS, COLUMNS), COLUMNS)
            right = jnp.concatenate([w_ref[HEADS * p + h, :, columns] for p in pieces], axis=0)
            product = jnp.dot(left, right, preferred_element_type=jnp.float32)
            if not begin:
                product += acc_ref[:, columns]
            if end:
                out_ref[:, columns] = product.astype(out_ref.dtype)
            else:
                acc_ref[:, columns] = product

    merge(0)
    forward(0)
    merge(1)
    weights.wait()
    multiply(0, core, True, False)
    gathered(0)
    multiply(0, 1 - core, False, False)
    forward(1)
    multiply(1, core, False, False)
    gathered(1)
    multiply(1, 1 - core, False, True)
    for copy in pending:
        copy.wait_send()


def finish(outs, logs, w_out):
    anywhere = pl.BlockSpec(memory_space=pl.ANY)
    dma = pltpu.SemaphoreType.DMA
    rows, width = 2 * HALF, w_out.shape[1]
    blocks = pltpu.with_memory_space_constraint(w_out.reshape(HEAD * HEADS, WIDTH, width), pltpu.HBM)
    return pl.pallas_call(
        finish_kernel,
        out_shape=jax.ShapeDtypeStruct((rows, width), outs.dtype),
        in_specs=[anywhere, anywhere, pl.BlockSpec(memory_space=pltpu.HBM)],
        out_specs=pl.BlockSpec(memory_space=pltpu.VMEM),
        scratch_shapes=[
            pltpu.VMEM((HEADS, CTX, WIDTH, HALF), outs.dtype),
            pltpu.VMEM(logs.shape, logs.dtype),
            pltpu.VMEM((HEADS, HEAD, rows, WIDTH), outs.dtype),
            pltpu.VMEM(blocks.shape, blocks.dtype),
            pltpu.VMEM((rows, width), jnp.float32),
            dma,
            dma((1 + HEADS,)),
            dma((HEADS, CTX)),
            dma((CTX,)),
            dma((HEADS, CTX)),
            dma((CTX,)),
            dma((HEADS, 2, 3)),
            dma((HEADS, 2, SIDE)),
            dma((HEADS, HEAD, 2)),
        ],
        compiler_params=pltpu.CompilerParams(collective_id=1, has_side_effects=True, vmem_limit_bytes=48 * 1024 * 1024),
        name="finish",
    )(outs, logs, blocks)


def body(*operands):
    w_out = operands[3]
    held = [pltpu.with_memory_space_constraint(array, pltpu.HBM) for array in operands if array is not w_out]
    queries, keys, values, new_counts, prior_lengths = held
    where = lax.axis_index("ctx").astype(jnp.int32).reshape(1)
    gathered, far_keys, far_turned, turned = dispatch(queries, keys, values)
    outs, logs = attend(where, new_counts, prior_lengths, gathered, keys, far_keys, turned, far_turned)
    return finish(outs, logs, w_out)


def solution(mesh):
    return jax.shard_map(
        body,
        mesh=mesh,
        in_specs=(P("ctx", "head"), P("ctx", None), P("ctx", None), P(None, "head"), P(), P()),
        out_specs=P("ctx", "head"),
        check_vma=False,
    )
```

```python
import functools
import math

import jax
import jax.numpy as jnp
from jax import lax
from jax.experimental import pallas as pl
from jax.experimental.pallas import tpu as pltpu
from jax.sharding import PartitionSpec as P

MESH = pl.DeviceIdType.MESH
CTX = 16
HEAD = 8
SIDE = 4
REQS = 8
HALF = 128
WIDTH = 128
HEADS = 2
LANES = HALF * HEADS
KEYS = 4096
PIECE = KEYS // HEAD
CHUNKS = 4
CHUNK = 2 * PIECE // CHUNKS
COLUMNS = 2048
FAR_FIRST = (
    (2, 2), (2, 1), (1, 2), (2, 3), (3, 2), (1, 1), (3, 3), (1, 3), (3, 1), (2, 0), (0, 2), (0, 1), (1, 0), (0, 3), (3, 0)
)
UNIT = 2048
PART = 1024
ALIGN = CHUNK
STEPS = CTX * (2 * KEYS // PART + 1) + 4
LOW = -1e9
NEG = -1e30
SCALE = math.log2(math.e) / math.sqrt(WIDTH)
VMEM = 56 * 1024 * 1024


def remote(src, dst, send, recv, ctx, head):
    return pltpu.make_async_remote_copy(
        src_ref=src, dst_ref=dst, send_sem=send, recv_sem=recv, device_id=(ctx, head), device_id_type=MESH
    )


def greet(peers):
    barrier = pltpu.get_barrier_semaphore()
    for ctx, head in peers:
        pl.semaphore_signal(barrier, inc=1, device_id=(ctx, head), device_id_type=MESH)


def meet(peers):
    pl.semaphore_wait(pltpu.get_barrier_semaphore(), len(peers))


def dispatch_kernel(
    q_any, k_ref, v_any, qt_ref, kf_ref, vf_ref, vo_ref, q_ref, v_ref, qs_ref, vs_ref,
    own_sem, qz_send, qx_send, q_recv, kz_send, ky_send, kc_send, k_recv,
):
    ctx, head = lax.axis_index("ctx"), lax.axis_index("head")
    z, x = ctx // SIDE, ctx % SIDE
    y, core = head // 2, head % 2
    far = lax.rem(ctx + CTX // 2, CTX)
    twin = y * 2 + (1 - core)

    def zed(d):
        return lax.rem(z + d, SIDE)

    def on_x(d):
        return lax.rem(x + d, SIDE)

    def on_y(d):
        return lax.rem(y + d, SIDE) * 2 + core

    peers = (
        [(zed(d) * SIDE + x, head) for d in (1, 2, 3)]
        + [(z * SIDE + on_x(d), head) for d in (1, 2, 3)]
        + [(ctx, on_y(d)) for d in (1, 2, 3)]
        + [(ctx, twin)]
    )
    greet(peers)
    loads = [
        pltpu.make_async_copy(q_any, q_ref, own_sem.at[0]),
        pltpu.make_async_copy(v_any, v_ref, own_sem.at[1]),
    ]
    for load in loads:
        load.start()
    loads[0].wait()
    for rows in range(2):
        for h in range(HEADS):
            block = q_ref[rows * HALF : (rows + 1) * HALF, h * WIDTH : (h + 1) * WIDTH]
            qs_ref[rows, :, h * HALF : (h + 1) * HALF] = block.T

    loads[1].wait()

    @pl.loop(0, KEYS // CHUNK)
    def _(p):
        vs_ref[p] = v_ref[pl.ds(pl.multiple_of(p * CHUNK, CHUNK), CHUNK), :].T

    meet(peers)
    pending = []

    def start(copy):
        copy.start()
        pending.append(copy)

    def number(p, c):
        return p * (PIECE // CHUNK) + c % 2

    def source(c):
        i = number(head, c)
        return k_ref.at[pl.ds(pl.multiple_of(i * CHUNK, CHUNK), CHUNK), :] if c < 2 else vs_ref.at[i]

    def chunk(p, c):
        i = number(p, c)
        return kf_ref.at[pl.ds(pl.multiple_of(i * CHUNK, CHUNK), CHUNK), :] if c < 2 else vf_ref.at[i]

    def share_q(slot, src, turn, ways):
        for d in ways:
            to = z * SIDE + on_x(d)
            start(remote(src, qt_ref.at[slot], qx_send.at[turn, d - 1], q_recv.at[slot], to, head))

    def arrived_q(slot):
        remote(qt_ref.at[slot], qt_ref.at[slot], qz_send.at[0], q_recv.at[slot], ctx, head).wait_recv()

    def pass_q(d):
        slot = zed(d) * SIDE + x
        arrived_q(slot)
        share_q(slot, qt_ref.at[slot], d, (1, 3, 2))

    def arrived_kv(p, c):
        ref = chunk(p, c)
        remote(ref, ref, kz_send.at[0], k_recv.at[p, c], ctx, head).wait_recv()

    def send_kv(p, c, sem, to):
        ref = chunk(p, c)
        start(remote(ref, ref, sem, k_recv.at[p, c], ctx, to))

    def pass_kv(c):
        arrived_kv(head, c)
        for d in (1, 3, 2):
            send_kv(head, c, ky_send.at[c, d - 1], on_y(d))
        send_kv(head, c, kc_send.at[0, c], twin)

    def relay_kv(c):
        for d in (1, 3):
            p = on_y(d)
            arrived_kv(p, c)
            send_kv(p, c, kc_send.at[d, c], twin)

    def last_kv(c):
        p = on_y(2)
        arrived_kv(p, c)
        send_kv(p, c, kc_send.at[2, c], twin)

    for c in range(CHUNKS):
        start(remote(source(c), chunk(head, c), kz_send.at[c], k_recv.at[head, c], far, head))
        if c == 0:
            for d in (1, 3):
                zt = zed(d)
                start(remote(qs_ref.at[zt // 2], qt_ref.at[ctx], qz_send.at[d - 1], q_recv.at[ctx], zt * SIDE + x, head))
        if c == 1:
            zt = zed(2)
            start(remote(qs_ref.at[zt // 2], qt_ref.at[ctx], qz_send.at[1], q_recv.at[ctx], zt * SIDE + x, head))
    share_q(ctx, qs_ref.at[z // 2], 0, (1, 3, 2))
    own = [
        pltpu.make_async_copy(qs_ref.at[z // 2], qt_ref.at[ctx], own_sem.at[0]),
        pltpu.make_async_copy(vs_ref, vo_ref, own_sem.at[1]),
    ]
    for copy in own:
        copy.start()

    pass_kv(0)
    pass_q(1)
    pass_q(3)
    pass_kv(1)
    pass_q(2)
    relay_kv(0)
    pass_kv(2)
    relay_kv(1)
    pass_kv(3)
    relay_kv(2)
    last_kv(0)
    relay_kv(3)
    last_kv(1)
    last_kv(2)
    last_kv(3)
    for d in range(SIDE):
        row = zed(d) * SIDE
        arrived_q(row + on_x(1))
        arrived_q(row + on_x(3))
        arrived_q(row + on_x(2))
    for c in range(CHUNKS):
        for d in range(SIDE):
            arrived_kv(lax.rem(y + d, SIDE) * 2 + (1 - core), c)
    for copy in own:
        copy.wait()
    for copy in pending:
        copy.wait_send()


def dispatch(queries, keys, values):
    anywhere = pl.BlockSpec(memory_space=pl.ANY)
    held = pl.BlockSpec(memory_space=pltpu.HBM)
    dma = pltpu.SemaphoreType.DMA
    return pl.pallas_call(
        dispatch_kernel,
        out_shape=(
            jax.ShapeDtypeStruct((CTX, WIDTH, LANES), queries.dtype),
            jax.ShapeDtypeStruct((KEYS, WIDTH), keys.dtype),
            jax.ShapeDtypeStruct((KEYS // CHUNK, WIDTH, CHUNK), values.dtype),
            jax.ShapeDtypeStruct((KEYS // CHUNK, WIDTH, CHUNK), values.dtype),
        ),
        in_specs=[held] * 3,
        out_specs=(anywhere,) * 4,
        scratch_shapes=[
            pltpu.VMEM(queries.shape, queries.dtype),
            pltpu.VMEM(values.shape, values.dtype),
            pltpu.VMEM((2, WIDTH, LANES), queries.dtype),
            pltpu.VMEM((KEYS // CHUNK, WIDTH, CHUNK), values.dtype),
            dma((2,)),
            dma((3,)),
            dma((SIDE, 3)),
            dma((CTX,)),
            dma((CHUNKS,)),
            dma((CHUNKS, 3)),
            dma((SIDE, CHUNKS)),
            dma((HEAD, CHUNKS)),
        ],
        compiler_params=pltpu.CompilerParams(collective_id=0, has_side_effects=True, vmem_limit_bytes=48 * 1024 * 1024),
        name="dispatch",
    )(queries, keys, values)


def attend_kernel(where_ref, new_ref, prior_ref, qt_any, k_any, kf_any, vo_any, vf_any, ot_ref, st_ref,
                  qt_ref, k_ref, vt_ref, s0_ref, s1_ref, x0_ref, x1_ref, m_ref, l_ref, acc_ref, tile_ref, pos_ref, part_ref, load_sem):
    ctx = where_ref[0]
    half = ctx // (CTX // 2)
    mine, other = pl.multiple_of(half * KEYS, KEYS), pl.multiple_of((1 - half) * KEYS, KEYS)
    blocks = KEYS // CHUNK
    loads = [
        pltpu.make_async_copy(src, dst, load_sem.at[i])
        for i, (src, dst) in enumerate(
            (
                (qt_any, qt_ref),
                (k_any, k_ref.at[pl.ds(mine, KEYS), :]),
                (kf_any, k_ref.at[pl.ds(other, KEYS), :]),
                (vo_any, vt_ref.at[pl.ds(half * blocks, blocks)]),
                (vf_any, vt_ref.at[pl.ds((1 - half) * blocks, blocks)]),
            )
        )
    ]
    for load in loads:
        load.start()
    base = lax.rem(ctx, CTX // 2) * KEYS

    q_start, k_start = [jnp.int32(0)], [jnp.int32(0)]
    for r in range(REQS - 1):
        q_start.append(q_start[-1] + new_ref[r])
        k_start.append(k_start[-1] + new_ref[r] + prior_ref[r])
    ahead = [prior_ref[r] + k_start[r] - q_start[r] for r in range(REQS)]
    lower = base
    upper = base + CTX // 2 * KEYS

    def bounds(row):
        lo, hi = jnp.zeros_like(row), jnp.full_like(row, ahead[0])
        for r in range(1, REQS):
            here = row >= q_start[r]
            lo = jnp.where(here, k_start[r], lo)
            hi = jnp.where(here, ahead[r], hi)
        return lo, row + hi

    def span(lo, hi):
        a0 = jnp.clip(lo - lower, 0, KEYS)
        e0 = jnp.clip(hi + 1 - lower, 0, KEYS)
        a1 = jnp.clip(lo - upper, 0, KEYS)
        e1 = jnp.clip(hi + 1 - upper, 0, KEYS)
        return jnp.where(e0 > a0, a0, KEYS + a1), jnp.where(e1 > a1, KEYS + e1, e0)

    def first_row(b):
        return b * (2 * HALF) + half * HALF

    def plan(b, count):
        lo_all, hi_one = bounds(first_row(b))
        lo_one, hi_all = bounds(first_row(b) + HALF - 1)
        begin, end = span(lo_all, hi_all)
        full_begin, full_end = span(lo_one, hi_one)
        full_end = jnp.where(hi_one >= lo_one, full_end, 0)

        def put(state):
            at, i = state
            full = (at >= full_begin) & (at + UNIT <= full_end)
            tile_ref[i] = b
            pos_ref[i] = at
            part_ref[i] = jnp.where(full, 0, 1)
            return at + jnp.where(full, UNIT, PART), i + 1

        return lax.while_loop(lambda state: state[0] < end, put, (begin // ALIGN * ALIGN, count))[1]

    ot_ref[...] = jnp.zeros_like(ot_ref)
    st_ref[...] = jnp.full(st_ref.shape, NEG, jnp.float32)
    acc_ref[...] = jnp.zeros_like(acc_ref)
    vt_ref[2 * blocks :] = jnp.zeros((PART // CHUNK, WIDTH, CHUNK), vt_ref.dtype)
    l_ref[...] = jnp.zeros_like(l_ref)
    m_ref[...] = jnp.full_like(m_ref, LOW)
    lane = lax.broadcasted_iota(jnp.int32, (1, LANES), 1) % HALF
    count = lax.fori_loop(0, CTX, plan, jnp.int32(0))
    for i in range(3):
        tile_ref[count + i] = jnp.int32(CTX)
        pos_ref[count + i] = jnp.int32(0)
        part_ref[count + i] = jnp.int32(1)

    def produce(i, s_ref, x_ref, part):
        size = PART if part else UNIT
        b = tile_ref[i]
        at = pl.multiple_of(pos_ref[i], ALIGN)
        s = jnp.dot(k_ref[pl.ds(at, size), :], qt_ref[jnp.minimum(b, CTX - 1)], preferred_element_type=jnp.float32) * SCALE
        if part:
            begin, end = span(*bounds(first_row(b) + lane))
            key = lax.broadcasted_iota(jnp.int32, (size, LANES), 0)
            s = jnp.where((key >= begin - at) & (key < end - at), s, NEG)
        s_ref[:size, :] = s
        x_ref[...] = jnp.max(s.reshape(size // 8, 8, LANES), axis=0)

    def process(i, s_ref, x_ref, part):
        size = PART if part else UNIT
        b = tile_ref[i]
        at = pl.multiple_of(pos_ref[i], ALIGN)
        first = tile_ref[jnp.maximum(i - 1, 0)] != b
        first = first | (i == 0)
        m_old = jnp.where(first, LOW, m_ref[0:1, :])
        m = jnp.maximum(m_old, jnp.max(x_ref[...], axis=0, keepdims=True))
        alpha = jnp.where(first, 0.0, jnp.exp2(m_old - m))
        p = jnp.exp2(s_ref[:size, :] - m)
        m_ref[...] = jnp.broadcast_to(m, m_ref.shape)
        l_ref[...] = l_ref[...] * alpha + jnp.sum(p.reshape(size // 8, 8, LANES), axis=0)
        p = p.astype(jnp.bfloat16)
        total = acc_ref[...] * alpha
        for j in range(size // CHUNK):
            total += jnp.dot(
                vt_ref[at // CHUNK + j], p[j * CHUNK : (j + 1) * CHUNK], preferred_element_type=jnp.float32
            )
        acc_ref[...] = total

    def finish(i):
        b = tile_ref[i]

        @pl.when((tile_ref[i + 1] != b) & (b < CTX))
        def _():
            total = jnp.sum(l_ref[...], axis=0, keepdims=True)
            live = total > 0.0
            safe = jnp.where(live, total, 1.0)
            log = jnp.where(live, m_ref[0:1, :] + jnp.log2(safe), NEG)
            out = (acc_ref[...] * (1.0 / safe)).astype(ot_ref.dtype)
            for h in range(HEADS):
                st_ref[b, h : h + 1, :] = log[:, h * HALF : (h + 1) * HALF]
                ot_ref[b, h] = out[:, h * HALF : (h + 1) * HALF]

    def step(i, now, later):
        for after in range(2):
            for before in range(2):

                @pl.when((part_ref[i + 1] == after) & (part_ref[i] == before))
                def _():
                    produce(i + 1, *later, after)
                    process(i, *now, before)

        finish(i)

    even, odd = (s0_ref, x0_ref), (s1_ref, x1_ref)
    for load in loads:
        load.wait()
    for after in range(2):

        @pl.when(part_ref[0] == after)
        def _():
            produce(0, *even, after)

    @pl.loop(0, (count + 1) // 2)
    def _(i):
        step(2 * i, even, odd)
        step(2 * i + 1, odd, even)


def attend(where, new_counts, prior_lengths, gathered, keys, far_keys, turned, far_turned):
    scalars = pl.BlockSpec(memory_space=pltpu.SMEM)
    vector = pl.BlockSpec(memory_space=pltpu.VMEM)
    return pl.pallas_call(
        attend_kernel,
        out_shape=(
            jax.ShapeDtypeStruct((CTX, HEADS, WIDTH, HALF), jnp.bfloat16),
            jax.ShapeDtypeStruct((CTX, 8, HALF), jnp.float32),
        ),
        in_specs=[scalars] * 3 + [pl.BlockSpec(memory_space=pl.ANY), pl.BlockSpec(memory_space=pltpu.HBM)] + [pl.BlockSpec(memory_space=pl.ANY)] * 3,
        out_specs=(vector, vector),
        scratch_shapes=[
            pltpu.VMEM(gathered.shape, gathered.dtype),
            pltpu.VMEM((2 * KEYS + PART, WIDTH), keys.dtype),
            pltpu.VMEM(((2 * KEYS + PART) // CHUNK, WIDTH, CHUNK), turned.dtype),
            pltpu.VMEM((UNIT, LANES), jnp.float32),
            pltpu.VMEM((UNIT, LANES), jnp.float32),
            pltpu.VMEM((8, LANES), jnp.float32),
            pltpu.VMEM((8, LANES), jnp.float32),
            pltpu.VMEM((8, LANES), jnp.float32),
            pltpu.VMEM((8, LANES), jnp.float32),
            pltpu.VMEM((WIDTH, LANES), jnp.float32),
            pltpu.SMEM((STEPS,), jnp.int32),
            pltpu.SMEM((STEPS,), jnp.int32),
            pltpu.SMEM((STEPS,), jnp.int32),
            pltpu.SemaphoreType.DMA((5,)),
        ],
        compiler_params=pltpu.CompilerParams(vmem_limit_bytes=48 * 1024 * 1024),
        name="attend",
    )(where, new_counts, prior_lengths, gathered, keys, far_keys, turned, far_turned)


def finish_kernel(
    ot_ref, st_ref, w_any, out_ref, og_ref, sg_ref, att_ref, w_ref, acc_ref,
    w_sem, own_sem, o_send, s_send, o_recv, s_recv, y_send, c_send, a_recv,
):
    ctx, head = lax.axis_index("ctx"), lax.axis_index("head")
    z, x = ctx // SIDE, ctx % SIDE
    y, core = head // 2, head % 2
    twin = y * 2 + (1 - core)

    def on_y(d):
        return lax.rem(y + d, SIDE) * 2 + core

    def at(steps):
        return lax.rem(z + steps[0], SIDE) * SIDE + lax.rem(x + steps[1], SIDE)

    peers = [(at(steps), head) for steps in FAR_FIRST] + [(ctx, on_y(d)) for d in (1, 2, 3)] + [(ctx, twin)]
    greet(peers)
    weights = pltpu.make_async_copy(w_any, w_ref, w_sem)
    weights.start()
    own = [pltpu.make_async_copy(st_ref.at[ctx], sg_ref.at[ctx], own_sem.at[0])]
    own += [pltpu.make_async_copy(ot_ref.at[ctx, h], og_ref.at[h, ctx], own_sem.at[1 + h]) for h in range(HEADS)]
    for copy in own:
        copy.start()
    meet(peers)
    pending = []

    def start(copy):
        copy.start()
        pending.append(copy)

    for i, steps in enumerate(FAR_FIRST):
        to = at(steps)
        start(remote(st_ref.at[to], sg_ref.at[ctx], s_send.at[i], s_recv.at[ctx], to, head))
        start(remote(ot_ref.at[to, 0], og_ref.at[0, ctx], o_send.at[0, i], o_recv.at[0, ctx], to, head))
    for h in range(1, HEADS):
        for i, steps in enumerate(FAR_FIRST):
            to = at(steps)
            start(remote(ot_ref.at[to, h], og_ref.at[h, ctx], o_send.at[h, i], o_recv.at[h, ctx], to, head))
    for copy in own:
        copy.wait()
    for steps in FAR_FIRST:
        of = at(steps)
        remote(sg_ref.at[of], sg_ref.at[of], s_send.at[0], s_recv.at[of], ctx, head).wait_recv()

    def share(h, p, r):
        return att_ref.at[h, p, pl.ds(r * HALF, HALF), :]

    def arrived(h, p, r):
        ref = share(h, p, r)
        remote(ref, ref, c_send.at[h, r, 0], a_recv.at[h, p, r], ctx, head).wait_recv()

    def send(h, p, r, sem, to):
        ref = share(h, p, r)
        start(remote(ref, ref, sem, a_recv.at[h, p, r], ctx, to))

    def merge(h):
        for steps in FAR_FIRST:
            of = at(steps)
            ref = og_ref.at[h, of]
            remote(ref, ref, o_send.at[h, 0], o_recv.at[h, of], ctx, head).wait_recv()
        for half in range(2):
            members = range(half * CTX // 2, (half + 1) * CTX // 2)
            logs = [sg_ref[i, h : h + 1, :] for i in members]
            top = functools.reduce(jnp.maximum, logs)
            shares = [jnp.exp2(log - top) for log in logs]
            inverse = 1.0 / functools.reduce(jnp.add, shares)
            out = jnp.zeros((WIDTH, HALF), jnp.float32)
            for i, part in zip(members, shares):
                out += og_ref[h, i].astype(jnp.float32) * (part * inverse)
            att_ref[h, head, half * HALF : (half + 1) * HALF, :] = out.T.astype(att_ref.dtype)
            for d in (2, 1, 3):
                send(h, head, half, y_send.at[h, half, d - 1], on_y(d))
            send(h, head, half, c_send.at[h, half, 0], twin)

    def forward(h):
        for r in range(2):
            for d in (1, 3, 2):
                p = on_y(d)
                arrived(h, p, r)
                send(h, p, r, c_send.at[h, r, d], twin)

    def gathered(h):
        for r in range(2):
            for d in range(SIDE):
                arrived(h, lax.rem(y + d, SIDE) * 2 + (1 - core), r)

    def multiply(h, side, begin, end):
        pieces = [lax.rem(y + d, SIDE) * 2 + side for d in range(SIDE)]
        left = jnp.concatenate([att_ref[h, p] for p in pieces], axis=1)

        @pl.loop(0, w_ref.shape[2] // COLUMNS)
        def _(n):
            columns = pl.ds(pl.multiple_of(n * COLUMNS, COLUMNS), COLUMNS)
            right = jnp.concatenate([w_ref[HEADS * p + h, :, columns] for p in pieces], axis=0)
            product = jnp.dot(left, right, preferred_element_type=jnp.float32)
            if not begin:
                product += acc_ref[:, columns]
            if end:
                out_ref[:, columns] = product.astype(out_ref.dtype)
            else:
                acc_ref[:, columns] = product

    merge(0)
    forward(0)
    merge(1)
    weights.wait()
    multiply(0, core, True, False)
    gathered(0)
    multiply(0, 1 - core, False, False)
    forward(1)
    multiply(1, core, False, False)
    gathered(1)
    multiply(1, 1 - core, False, True)
    for copy in pending:
        copy.wait_send()


def finish(outs, logs, w_out):
    anywhere = pl.BlockSpec(memory_space=pl.ANY)
    dma = pltpu.SemaphoreType.DMA
    rows, width = 2 * HALF, w_out.shape[1]
    blocks = pltpu.with_memory_space_constraint(w_out.reshape(HEAD * HEADS, WIDTH, width), pltpu.HBM)
    return pl.pallas_call(
        finish_kernel,
        out_shape=jax.ShapeDtypeStruct((rows, width), outs.dtype),
        in_specs=[anywhere, anywhere, pl.BlockSpec(memory_space=pltpu.HBM)],
        out_specs=pl.BlockSpec(memory_space=pltpu.VMEM),
        scratch_shapes=[
            pltpu.VMEM((HEADS, CTX, WIDTH, HALF), outs.dtype),
            pltpu.VMEM(logs.shape, logs.dtype),
            pltpu.VMEM((HEADS, HEAD, rows, WIDTH), outs.dtype),
            pltpu.VMEM(blocks.shape, blocks.dtype),
            pltpu.VMEM((rows, width), jnp.float32),
            dma,
            dma((1 + HEADS,)),
            dma((HEADS, CTX)),
            dma((CTX,)),
            dma((HEADS, CTX)),
            dma((CTX,)),
            dma((HEADS, 2, 3)),
            dma((HEADS, 2, SIDE)),
            dma((HEADS, HEAD, 2)),
        ],
        compiler_params=pltpu.CompilerParams(collective_id=1, has_side_effects=True, vmem_limit_bytes=48 * 1024 * 1024),
        name="finish",
    )(outs, logs, blocks)


def body(*operands):
    w_out = operands[3]
    held = [pltpu.with_memory_space_constraint(array, pltpu.HBM) for array in operands if array is not w_out]
    queries, keys, values, new_counts, prior_lengths = held
    where = lax.axis_index("ctx").astype(jnp.int32).reshape(1)
    gathered, far_keys, far_turned, turned = dispatch(queries, keys, values)
    outs, logs = attend(where, new_counts, prior_lengths, gathered, keys, far_keys, turned, far_turned)
    return finish(outs, logs, w_out)


def solution(mesh):
    return jax.shard_map(
        body,
        mesh=mesh,
        in_specs=(P("ctx", "head"), P("ctx", None), P("ctx", None), P(None, "head"), P(), P()),
        out_specs=P("ctx", "head"),
        check_vma=False,
    )
```
